32 devices in a mesh: groups: 2 (over x), out: 16 (over z, y, core).
Axes of the slice: x: 2, y: 2, z: 4, core: 2. Of those that a mesh axis runs over, the one named last changes fastest.
Arguments:
- stream: bfloat16 [128, 12288], P('groups', 'out'), parts along dimension 0, may hold values from -6 to 6
- norm_gain: float32 [12288], replicated, may hold values from 0.5 to 1.5
- w_query: bfloat16 [12288, 6144], P(None, 'out')
- w_keyval: bfloat16 [12288, 1024], P(None, 'out'), may hold values from -0.0546875 to 0.0546875
- w_out: bfloat16 [6144, 12288], P('out'), may hold values from -0.75 to 0.75
- lengths: int32 [128], P(('groups', 'out')), parts along dimension 0, may hold values from 1 to 512, as said below
- key_cache: bfloat16 [128, 512, 512], P(('groups', 'out')), parts along dimension 0, may hold values from -127 to 127, as said below
- value_cache: bfloat16 [128, 512, 512], P(('groups', 'out')), parts along dimension 0, may hold values from -127 to 127, as said below
- key_scales: int32 [128, 4, 4], P(('groups', 'out')), parts along dimension 0, may hold values from -8 to -6
- value_scales: int32 [128, 4, 4], P(('groups', 'out')), parts along dimension 0, may hold values from -8 to -6
Outputs:
- new_stream: bfloat16 [128, 12288], P('groups', 'out'), parts along dimension 0
The draws below stay inside these ranges and needn't reach their ends.
There are 2 independent parts, one for each index of `groups`. The reference program is written for one: setup_inputs(seed, part) draws one part's arguments, and reference() takes and returns one part's arrays. A program takes and returns all parts, laid end to end along the dimension named above; an argument that names none is the same for every part. Nothing has to cross between parts.
Inputs may be any that keep to these rules, and one draw needn't show every extreme that they name: `lengths`: every row holds at least one earlier token; in every draw some row holds exactly 512. `key_cache`: whole numbers, codes of an eight-bit cache. `value_cache`: whole numbers, codes of an eight-bit cache.
All inputs are finite; a program needn't handle non-finite values.
Results may differ from the reference program's by a relative error of at most 0.024.
The reference program's roundings to bfloat16 on the way count: a program that leaves them out, or rounds other values in their place, can miss the bound.
Values may be sent and summed in bfloat16 or wider, within the bound.
A program may use at most 64 MiB of HBM per device.

```python
import math
import jax
import jax.numpy as jnp
from jax import lax

D = 12288
HQ = 48
KVH = 4
HD = 128
CAP = 512
ROWS = 64
GRP = 12
NB = 4


def draw_lengths(key, part):
    first, second, third = jax.random.split(key, 3)
    base = jax.random.randint(first, (ROWS,), 1, CAP + 1)
    coin = jax.random.randint(second, (ROWS,), 0, 4)
    lens = jnp.where(coin == 0, base, base // 4 + 1)
    chosen = jax.random.randint(third, (), 0, ROWS)
    lens = jnp.where(jnp.arange(ROWS) == chosen, CAP, lens)
    return lens.astype(jnp.int32)


def draw_codes(key):
    first = jax.random.fold_in(key, 0)
    codes = jax.random.randint(first, (ROWS, CAP, KVH * HD), -127, 128)
    return codes.astype(jnp.float32).astype(jnp.bfloat16)


def draw_key_cache(key, part):
    return draw_codes(jax.random.fold_in(key, 11))


def draw_value_cache(key, part):
    return draw_codes(jax.random.fold_in(key, 23))


def draw_w_query(key, part):
    first, second, third, fourth = jax.random.split(jax.random.fold_in(key, 37), 4)
    base = jax.random.truncated_normal(first, -4.0, 4.0, (D, HQ * HD), jnp.float32)
    strength = jax.random.uniform(third, (HQ,), jnp.float32, 48.0, 96.0)
    coin = jax.random.randint(second, (HQ,), 0, 6)
    forced = jax.random.randint(fourth, (), 0, HQ)
    heads = jnp.arange(HQ)
    boosted = jnp.logical_or(coin == 0, heads == forced)
    factor = jnp.where(boosted, strength, 1.0)
    column_factor = jnp.repeat(factor, HD)
    return (base * column_factor[None, :] * D ** (-0.5)).astype(jnp.bfloat16)


def set_ends(drawn, own_key, least, largest):
    longest = drawn.shape.index(max(drawn.shape))
    spots = []
    for shift in (0, 1):
        where = [jax.random.randint(jax.random.fold_in(own_key, axis), (), 0, length) for axis, length in enumerate(drawn.shape)]
        where[longest] = (where[longest] + shift) % drawn.shape[longest]
        spots.append(tuple(where))
    return drawn.at[spots[0]].set(least).at[spots[1]].set(largest)


def with_spikes(values, own_key, source, target, parts, factor):
    def block_of(dim):
        return (jnp.arange(values.shape[dim]) // (values.shape[dim] // parts)).reshape((-1,) + (1,) * (values.ndim - 1 - dim))

    first = jax.random.permutation(own_key, parts)[block_of(target)]
    other_side = (block_of(target) + parts // 2) % parts
    return jnp.where((block_of(source) == first) | (block_of(source) == other_side), factor * values, values)


def steps_of(stream_key, shape, cuts, low, high):
    def one(dim, parts):
        draws = jax.random.uniform(jax.random.fold_in(jax.random.fold_in(stream_key, 6), dim), (parts,), jnp.float32, low / len(cuts), high / len(cuts))
        return jnp.repeat(jnp.exp(draws), shape[dim] // parts).reshape((-1,) + (1,) * (len(shape) - dim - 1))

    gain = one(*cuts[0])
    for cut in cuts[1:]:
        gain = gain * one(*cut)
    return gain


def normal_values(stream_key, extent, deviation, limit, cuts=(), held_as=jnp.bfloat16):
    level = steps_of(stream_key, extent, cuts, -0.22, 0.18) if cuts else 1.0
    entries = jax.random.normal(stream_key, extent, jnp.float32) * deviation * level
    return jnp.minimum(jnp.maximum(entries, -limit), limit).astype(held_as)


def gaussian_with(stream_key, extent, deviation, limit, shards, heavy, held_as=jnp.bfloat16):
    array = deviation * jax.random.normal(stream_key, extent, jnp.float32)
    if shards:
        array = array * steps_of(stream_key, extent, shards, -0.22, 0.18)
    return jnp.clip(with_spikes(array, jax.random.fold_in(stream_key, 3), *heavy), -limit, limit).astype(held_as)


def setup_inputs(seed: int = 0, part: int = 0) -> dict:
    splits = jax.random.split(jax.random.key(seed), 11)
    part_keys = jax.random.split(jax.random.fold_in(splits[10], part), 11)
    return {
        "stream": normal_values(part_keys[0], (ROWS, D), 1.0, 6.0, ((1, 16),)),
        "norm_gain": jnp.clip(1.0 + 0.1 * jax.random.normal(splits[1], (D,), jnp.float32), 0.5, 1.5),
        "w_query": draw_w_query(jax.random.fold_in(splits[10], 71), part),
        "w_keyval": normal_values(splits[3], (D, 2 * KVH * HD), D ** -0.5, 0.0546875, ((1, 16),)),
        "w_out": gaussian_with(splits[4], (HQ * HD, D), HD ** -0.5, 0.75, ((0, 16),), (0, 1, 16, 2.0)),
        "lengths": draw_lengths(jax.random.fold_in(jax.random.fold_in(splits[10], part), 71), part),
        "key_cache": draw_key_cache(jax.random.fold_in(jax.random.fold_in(splits[10], part), 71), part),
        "value_cache": draw_value_cache(jax.random.fold_in(jax.random.fold_in(splits[10], part), 71), part),
        "key_scales": set_ends(jax.random.randint(part_keys[8], (ROWS, NB, KVH), -8, -5), jax.random.fold_in(part_keys[8], 1), -8, (-5) - 1).astype(jnp.int32),
        "value_scales": set_ends(jax.random.randint(part_keys[9], (ROWS, NB, KVH), -8, -5), jax.random.fold_in(part_keys[9], 1), -8, (-5) - 1).astype(jnp.int32),
    }


rope_base = 1000000.0
norm_eps = 1e-05

def rotate(vec, position):
    half = vec.shape[-1] // 2
    index = jnp.arange(half, dtype=jnp.float32)
    freq = jnp.exp(index * (-2.0 * math.log(rope_base) / vec.shape[-1]))
    angle = position * freq
    cosine = jnp.cos(angle)
    sine = jnp.sin(angle)
    first = vec[..., :half]
    second = vec[..., half:]
    return jnp.concatenate([first * cosine - second * sine, second * cosine + first * sine], axis=-1)

def dequant(cache, scales):
    rows, span, width = cache.shape
    blocks = scales.shape[1]
    factor = jnp.exp2(scales.astype(jnp.float32)).astype(jnp.bfloat16)
    shaped = cache.reshape(rows, blocks, span // blocks, KVH, width // KVH)
    return (shaped * factor[:, :, None, :, None]).reshape(rows, span, KVH, width // KVH)

def reference(stream, norm_gain, w_query, w_keyval, w_out, lengths, key_cache, value_cache, key_scales, value_scales):
    xf = stream.astype(jnp.float32)
    meansq = lax.optimization_barrier(jnp.mean(xf * xf, axis=-1, keepdims=True))
    normed = (xf * lax.rsqrt(meansq + norm_eps) * norm_gain).astype(jnp.bfloat16)
    query = jnp.dot(normed, w_query, preferred_element_type=jnp.float32).astype(jnp.bfloat16)
    keyval = jnp.dot(normed, w_keyval, preferred_element_type=jnp.float32).astype(jnp.bfloat16)
    position = lengths.astype(jnp.float32)[:, None, None]
    rotated = rotate(query.astype(jnp.float32).reshape(ROWS, HQ, HD), position).astype(jnp.bfloat16)
    rotated = rotated.reshape(ROWS, KVH, GRP, HD).astype(jnp.float32)
    new_key = rotate(keyval[:, :KVH * HD].astype(jnp.float32).reshape(ROWS, KVH, HD), position).astype(jnp.bfloat16)
    new_value = keyval[:, KVH * HD:].reshape(ROWS, KVH, HD)
    keys = dequant(key_cache, key_scales).astype(jnp.float32)
    values = dequant(value_cache, value_scales).astype(jnp.float32)
    factor = HD ** (-0.5)
    scores = jnp.einsum('rkgd,rjkd->rkgj', rotated, keys) * factor
    valid = jnp.arange(CAP, dtype=jnp.int32)[None, :] < lengths[:, None]
    scores = jnp.where(valid[:, None, None, :], scores, -jnp.inf)
    own = jnp.einsum('rkgd,rkd->rkg', rotated, new_key.astype(jnp.float32)) * factor
    top = jnp.maximum(lax.optimization_barrier(jnp.max(scores, axis=-1)), own)
    weights = jnp.exp(scores - top[..., None])
    own_weight = jnp.exp(own - top)
    total = lax.optimization_barrier(jnp.sum(weights, axis=-1)) + own_weight
    rounded = weights.astype(jnp.bfloat16).astype(jnp.float32)
    own_rounded = lax.optimization_barrier(own_weight.astype(jnp.bfloat16)).astype(jnp.float32)
    summed = jnp.einsum('rkgj,rjkd->rkgd', rounded, values)
    summed = summed + own_rounded[..., None] * new_value.astype(jnp.float32)[:, :, None, :]
    attended = (summed / total[..., None]).astype(jnp.bfloat16).reshape(ROWS, HQ * HD)
    projected = jnp.dot(attended, w_out, preferred_element_type=jnp.float32)
    return (xf + projected).astype(jnp.bfloat16)
```

```python
import functools
import math

import jax
import jax.numpy as jnp
from jax import lax
from jax.experimental import pallas as pl
from jax.experimental.pallas import tpu as pltpu
from jax.sharding import PartitionSpec as P

HQ = 48
KVH = 4
HD = 128


rope_base = 1000000.0
norm_eps = 1e-05


def rotate(vec, position):
    half = vec.shape[-1] // 2
    index = jnp.arange(half, dtype=jnp.float32)
    freq = jnp.exp(index * (-2.0 * math.log(rope_base) / vec.shape[-1]))
    angle = position * freq
    cosine = jnp.cos(angle)
    sine = jnp.sin(angle)
    first = vec[..., :half]
    second = vec[..., half:]
    return jnp.concatenate(
        [first * cosine - second * sine, second * cosine + first * sine], axis=-1
    )


def dequant(cache, scales):
    rows, span, width = cache.shape
    blocks = scales.shape[1]
    factor = jnp.exp2(scales.astype(jnp.float32)).astype(jnp.bfloat16)
    shaped = cache.reshape(rows, blocks, span // blocks, KVH, width // KVH)
    return (shaped * factor[:, :, None, :, None]).reshape(rows, span, KVH, width // KVH)


def plain_device(
    stream,
    norm_gain,
    w_query,
    w_keyval,
    w_out,
    lengths,
    key_cache,
    value_cache,
    key_scales,
    value_scales,
):
    local_rows = lengths.shape[0]
    xf = stream.astype(jnp.float32)
    whole = lax.all_gather(stream, "out", axis=1, tiled=True).astype(jnp.float32)
    meansq = jnp.mean(whole * whole, axis=-1, keepdims=True)
    normed = (whole * lax.rsqrt(meansq + norm_eps) * norm_gain).astype(jnp.bfloat16)
    q_local = jnp.dot(normed, w_query, preferred_element_type=jnp.float32).astype(jnp.bfloat16)
    kv_local = jnp.dot(normed, w_keyval, preferred_element_type=jnp.float32).astype(jnp.bfloat16)
    q_rows, kv_rows = (
        lax.all_to_all(q_local, "out", split_axis=0, concat_axis=1, tiled=True),
        lax.all_to_all(kv_local, "out", split_axis=0, concat_axis=1, tiled=True),
    )
    position = lengths.astype(jnp.float32)[:, None, None]
    rotated = rotate(q_rows.astype(jnp.float32).reshape(local_rows, HQ, HD), position).astype(
        jnp.bfloat16
    )
    rotated = rotated.reshape(local_rows, KVH, HQ // KVH, HD)
    new_key = rotate(
        kv_rows[:, : KVH * HD].astype(jnp.float32).reshape(local_rows, KVH, HD), position
    ).astype(jnp.bfloat16)
    new_value = kv_rows[:, KVH * HD :].reshape(local_rows, KVH, HD)
    factor = HD ** (-0.5)
    own = jnp.einsum("rkgd,rkd->rkg", rotated, new_key, preferred_element_type=jnp.float32) * factor
    span = key_cache.shape[1]
    scores = (
        jnp.einsum(
            "rkgd,rjkd->rkgj",
            rotated,
            dequant(key_cache, key_scales),
            preferred_element_type=jnp.float32,
        )
        * factor
    )
    valid = jnp.arange(span, dtype=jnp.int32)[None, :] < lengths[:, None]
    scores = jnp.where(valid[:, None, None, :], scores, -jnp.inf)
    top = jnp.maximum(jnp.max(scores, axis=-1), own)
    weights = jnp.exp(scores - top[..., None])
    own_weight = jnp.exp(own - top)
    total = jnp.sum(weights, axis=-1) + own_weight
    own_rounded = lax.optimization_barrier(own_weight.astype(jnp.bfloat16)).astype(jnp.float32)
    summed = jnp.einsum(
        "rkgj,rjkd->rkgd",
        weights.astype(jnp.bfloat16),
        dequant(value_cache, value_scales),
        preferred_element_type=jnp.float32,
    )
    summed = summed + own_rounded[..., None] * new_value.astype(jnp.float32)[:, :, None, :]
    attended = (summed / total[..., None]).astype(jnp.bfloat16).reshape(local_rows, HQ * HD)
    heads = lax.all_to_all(attended, "out", split_axis=1, concat_axis=0, tiled=True)
    partial_terms = jnp.dot(heads, w_out, preferred_element_type=jnp.float32)
    projected = lax.psum_scatter(partial_terms, "out", scatter_dimension=1, tiled=True)
    return (xf + projected).astype(jnp.bfloat16)


MESH = pl.DeviceIdType.MESH
F32 = jnp.float32
BF16 = jnp.bfloat16
CONTRACT_LAST = (((1,), (1,)), ((), ()))


def fused_kernel(
    n, rows, width, local_rows, span,
    x_ref, gain_ref, cos_ref, sin_ref, len_ref, kfac_ref, vfac_ref,
    wq_hbm, wkv_hbm, wo_hbm, kc_hbm, vc_hbm,
    out_ref,
    wq, wkv, wo, kc, vc, xbuf, ssend, sbuf, accq, acckv, pk, qsend, qbuf, asend, abuf, heads,
    core_sb, core_rb, y_sb, y_rb, z_sb, up_rb, dn_rb, heads_sum,
    wq_sem, wo_sem, w_sem,
    ag_recv, ag_up, ag_dn, ag_y, ag_core,
    ss_send, ss_recv, q_send, q_recv, a_send, a_recv,
    core_send, core_recv, y_send, y_recv, z_send, up_recv, dn_recv,
):
    line = n // 4
    qcols = wq.shape[1]
    own_heads = qcols // HD
    tile = qbuf.shape[1]
    per_head = n // KVH
    qrows = per_head * tile
    me = lax.axis_index("out")
    grp = lax.axis_index("groups")
    a = me // 4
    b = (me // 2) % 2
    c = me % 2

    def at(pos, bb, cc):
        return (pos * 2 + bb) * 2 + cc

    up, down = at(a + 1, b, c), at(a - 1, b, c)
    ypeer, cpeer = at(a, 1 - b, c), at(a, b, 1 - c)
    low, high = a, line - 1 - a
    least = jnp.minimum(low, high)

    def ranked(m):
        d = (m + 1) // 2
        near = jnp.where(m % 2 == 1, a - d, a + d)
        far = jnp.where(high > low, a + (m - least), a - (m - least))
        return jnp.where(m <= 2 * least, near, far)

    def remote(src, dst, ssem, rsem, to):
        return pltpu.make_async_remote_copy(
            src_ref=src, dst_ref=dst, send_sem=ssem, recv_sem=rsem,
            device_id=(grp, to), device_id_type=MESH,
        )

    def wq_copy(i):
        at_rows = pl.ds(pl.multiple_of(i * width, width), width)
        return pltpu.make_async_copy(wq_hbm.at[at_rows], wq.at[at_rows], wq_sem.at[i])

    wo_parts = wo_sem.shape[0]
    wo_rows = wo.shape[0] // wo_parts

    def wo_copy(i):
        at_rows = pl.ds(i * wo_rows, wo_rows)
        return pltpu.make_async_copy(wo_hbm.at[at_rows], wo.at[at_rows], wo_sem.at[i])

    wkv_copy = pltpu.make_async_copy(wkv_hbm, wkv, w_sem.at[0])
    kc_copy = pltpu.make_async_copy(kc_hbm, kc, w_sem.at[1])
    vc_copy = pltpu.make_async_copy(vc_hbm, vc, w_sem.at[2])

    barrier = pltpu.get_barrier_semaphore()

    def others(body):
        def step(i, carry):
            body(lax.rem(me + i, n))
            return carry
        lax.fori_loop(1, n, step, 0)

    others(lambda o: pl.semaphore_signal(barrier, inc=1, device_id=(grp, o), device_id_type=MESH))

    wkv_copy.start()

    def start_wq(i, carry):
        wq_copy(lax.rem(me + i, n)).start()
        return carry
    lax.fori_loop(0, n, start_wq, 0)
    kc_copy.start()
    vc_copy.start()
    for i in range(wo_parts):
        wo_copy(i).start()

    xbuf[me] = x_ref[...]
    xf = x_ref[...].astype(F32)
    square = jnp.sum(xf * xf, axis=1, keepdims=True)
    spread = jnp.transpose(jnp.broadcast_to(square, (rows, 128)))
    ssend[...] = jnp.zeros_like(ssend)
    ssend[:, 0:rows] = spread[0:8, :]
    sbuf[me] = ssend[...]
    accq[...] = jnp.zeros_like(accq)
    acckv[...] = jnp.zeros_like(acckv)

    pl.semaphore_wait(barrier, n - 1)

    def ag_copy(block, ssem, to):
        return remote(xbuf.at[block], xbuf.at[block], ssem, ag_recv.at[block], to)

    def ag_wait(block):
        ag_copy(block, ag_core.at[0], cpeer).wait_recv()

    def spread_line(pos):
        block = at(pos, b, c)

        @pl.when((pos <= a) & (a < line - 1))
        def _():
            ag_copy(block, ag_up.at[pos], up).start()

        @pl.when((pos >= a) & (a > 0))
        def _():
            ag_copy(block, ag_dn.at[pos], down).start()

        ag_copy(block, ag_y.at[pos], ypeer).start()
        ag_copy(block, ag_core.at[pos], cpeer).start()

    def ss_copy(o, slot):
        return remote(ssend, sbuf.at[slot], ss_send.at[o], ss_recv.at[slot], o)

    others(lambda o: ss_copy(o, me).start())
    spread_line(a)
    others(lambda o: ss_copy(o, o).wait_recv())
    total_sq = jnp.sum(sbuf[...], axis=0)[0:1, :]
    column = jnp.transpose(jnp.broadcast_to(total_sq, (128, 128)))[0:rows, 0:1]
    scale = lax.rsqrt(column * (1.0 / (n * width)) + norm_eps)
    wkv_copy.wait()

    def project(block):
        wq_copy(block).wait()
        start = pl.multiple_of(block * width, width)
        normed = (xbuf[block].astype(F32) * scale * gain_ref[:, pl.ds(start, width)]).astype(BF16)
        accq[...] += jnp.dot(normed, wq[pl.ds(start, width), :], preferred_element_type=F32)
        acckv[...] += lax.dot_general(
            normed, wkv[:, pl.ds(start, width)], CONTRACT_LAST, preferred_element_type=F32
        )

    project(me)

    def gather_step(m, carry):
        @pl.when(m < line)
        def _():
            pos = ranked(m)
            ag_wait(at(pos, b, c))
            spread_line(pos)

        prev = ranked(m - 1)
        yblock = at(prev, 1 - b, c)
        ag_wait(yblock)
        ag_copy(yblock, ag_core.at[line + prev], cpeer).start()

        @pl.when(m < line)
        def _():
            project(at(ranked(m), b, c))

        project(yblock)
        cblock = at(prev, b, 1 - c)
        ag_wait(cblock)
        project(cblock)
        return carry
    lax.fori_loop(1, line + 1, gather_step, 0)

    def gather_last(m, carry):
        block = at(ranked(m), 1 - b, 1 - c)
        ag_wait(block)
        project(block)
        return carry
    lax.fori_loop(0, line, gather_last, 0)

    kv_cols = wkv.shape[0]
    pk[...] = jnp.zeros_like(pk)
    q_all = accq[...]
    kv_all = acckv[...]
    for j in range(n):
        mine = slice(j * local_rows, (j + 1) * local_rows)
        for g in range(own_heads):
            pk[j, g * local_rows:(g + 1) * local_rows, :] = q_all[mine, g * HD:(g + 1) * HD]
        pk[j, own_heads * local_rows:tile, 0:kv_cols] = kv_all[mine, :]
    qsend[...] = pk[...].astype(BF16)

    def q_copy(o, slot):
        return remote(qsend.at[o], qbuf.at[slot], q_send.at[o], q_recv.at[slot], o)

    others(lambda o: q_copy(o, me).start())
    qbuf[me] = qsend[me]

    ridx = lax.broadcasted_iota(jnp.int32, (qrows, 128), 0) % local_rows
    pick = lax.broadcasted_iota(jnp.int32, (qrows, tile), 0) % local_rows
    pick = pick + own_heads * local_rows == lax.broadcasted_iota(jnp.int32, (qrows, tile), 1)
    pick = pick.astype(F32).astype(BF16)
    blocks = span // 128

    def by_row(values):
        res = jnp.full((qrows, 128), values[0])
        for r in range(1, local_rows):
            res = jnp.where(ridx == r, values[r], res)
        return res

    limit = by_row([len_ref[r] for r in range(local_rows)])
    lane = lax.broadcasted_iota(jnp.int32, (qrows, 128), 1)
    cosine, sine = cos_ref[...], sin_ref[...]

    def rotated(v):
        return (v * cosine + pltpu.roll(v, HD // 2, 1) * sine).astype(BF16)

    kc_copy.wait()
    vc_copy.wait()
    others(lambda o: q_copy(o, o).wait_recv())

    pieces = HD // kv_cols
    factor = HD ** (-0.5)

    def new_head(first):
        res = None
        for p in range(pieces):
            part = jnp.dot(pick, qbuf[first + p], preferred_element_type=F32)
            part = part if p == 0 else pltpu.roll(part, p * kv_cols, 1)
            res = part if res is None else res + part
        return res

    for k in range(KVH):
        at_k = slice(k * HD, (k + 1) * HD)
        query = rotated(qbuf[k * per_head:(k + 1) * per_head].astype(F32).reshape(qrows, HD))
        new_key = rotated(new_head(k * pieces)).astype(F32)
        new_value = new_head((KVH + k) * pieces)
        own = jnp.sum(query.astype(F32) * new_key, axis=1, keepdims=True) * factor
        score = None
        for r in range(local_rows):
            one = lax.dot_general(query, kc[r, :, at_k], CONTRACT_LAST, preferred_element_type=F32)
            cut = [one[:, 128 * u:128 * (u + 1)] for u in range(blocks)]
            score = cut if r == 0 else [jnp.where(ridx == r, x, y) for x, y in zip(cut, score)]
        top = own
        for u in range(blocks):
            scales = by_row([kfac_ref[(r * blocks + u) * KVH + k] for r in range(local_rows)])
            score[u] = jnp.where(lane + 128 * u < limit, score[u] * scales * factor, -jnp.inf)
            top = jnp.maximum(top, jnp.max(score[u], axis=1, keepdims=True))
        own_weight = jnp.exp(own - top)
        total = own_weight
        weights = []
        for u in range(blocks):
            weight = jnp.exp(score[u] - top)
            total = total + jnp.sum(weight, axis=1, keepdims=True)
            scales = by_row([vfac_ref[(r * blocks + u) * KVH + k] for r in range(local_rows)])
            weights.append((weight.astype(BF16).astype(F32) * scales).astype(BF16))
        weights = jnp.concatenate(weights, axis=1)
        summed = None
        for r in range(local_rows):
            one = jnp.dot(weights, vc[r, :, at_k], preferred_element_type=F32)
            summed = one if r == 0 else jnp.where(ridx == r, one, summed)
        summed = summed + own_weight.astype(BF16).astype(F32) * new_value
        result = (summed / total).astype(BF16)
        for s in range(per_head):
            asend[k * per_head + s] = result[s * tile:(s + 1) * tile, :]

    def a_copy(o, slot):
        return remote(asend.at[o], abuf.at[slot], a_send.at[o], a_recv.at[slot], o)

    others(lambda o: a_copy(o, me).start())
    abuf[me] = asend[me]
    for i in range(wo_parts):
        wo_copy(i).wait()
    others(lambda o: a_copy(o, o).wait_recv())
    pk[...] = abuf[...].astype(F32)
    for j in range(n):
        for g in range(own_heads):
            heads[j * local_rows:(j + 1) * local_rows, g * HD:(g + 1) * HD] = (
                pk[j, g * local_rows:(g + 1) * local_rows, :]
            )
    attended = heads[...].astype(BF16)

    def partial(block):
        start = pl.multiple_of(block * width, width)
        return jnp.dot(attended, wo[:, pl.ds(start, width)], preferred_element_type=F32)

    def core_copy(slot):
        return remote(core_sb.at[slot], core_rb.at[slot], core_send.at[slot], core_recv.at[slot], cpeer)

    def y_copy(pos):
        return remote(y_sb.at[pos], y_rb.at[pos], y_send.at[pos], y_recv.at[pos], ypeer)

    def up_copy(pos):
        return remote(z_sb.at[pos], up_rb.at[pos], z_send.at[pos], up_recv.at[pos], up)

    def dn_copy(pos):
        return remote(z_sb.at[pos], dn_rb.at[pos], z_send.at[pos], dn_recv.at[pos], down)

    def loop_far(body):
        def step(m, carry):
            body(ranked(line - 1 - m))
            return carry
        lax.fori_loop(0, line, step, 0)

    def to_core_far(pos):
        core_sb[line + pos] = partial(at(pos, 1 - b, 1 - c)).astype(BF16)
        core_copy(line + pos).start()

    def to_pair(pos):
        term = partial(at(pos, 1 - b, c))
        core_copy(line + pos).wait_recv()
        y_sb[pos] = (term + core_rb[line + pos].astype(F32)).astype(BF16)
        y_copy(pos).start()

    def to_core_near(pos):
        core_sb[pos] = partial(at(pos, b, 1 - c)).astype(BF16)
        core_copy(pos).start()

    def to_line(pos):
        term = partial(at(pos, b, c))
        core_copy(pos).wait_recv()
        term = term + core_rb[pos].astype(F32)
        y_copy(pos).wait_recv()
        term = term + y_rb[pos].astype(F32)
        heads_sum[...] = term

        @pl.when((pos >= a) & (a > 0))
        def _():
            up_copy(pos).wait_recv()
            heads_sum[...] += up_rb[pos].astype(F32)

        @pl.when((pos <= a) & (a < line - 1))
        def _():
            dn_copy(pos).wait_recv()
            heads_sum[...] += dn_rb[pos].astype(F32)

        @pl.when(pos > a)
        def _():
            z_sb[pos] = heads_sum[...].astype(BF16)
            up_copy(pos).start()

        @pl.when(pos < a)
        def _():
            z_sb[pos] = heads_sum[...].astype(BF16)
            dn_copy(pos).start()

        @pl.when(pos == a)
        def _():
            out_ref[...] = (x_ref[...].astype(F32) + heads_sum[...]).astype(BF16)

    loop_far(to_core_far)
    loop_far(to_pair)
    loop_far(to_core_near)
    loop_far(to_line)

    def sent(pos, carry):
        block = at(pos, b, c)

        @pl.when((pos <= a) & (a < line - 1))
        def _():
            ag_copy(block, ag_up.at[pos], up).wait_send()

        @pl.when((pos >= a) & (a > 0))
        def _():
            ag_copy(block, ag_dn.at[pos], down).wait_send()

        ag_copy(block, ag_y.at[pos], ypeer).wait_send()
        ag_copy(block, ag_core.at[pos], cpeer).wait_send()
        ag_copy(at(pos, 1 - b, c), ag_core.at[line + pos], cpeer).wait_send()
        core_copy(pos).wait_send()
        core_copy(line + pos).wait_send()
        y_copy(pos).wait_send()

        @pl.when(pos > a)
        def _():
            up_copy(pos).wait_send()

        @pl.when(pos < a)
        def _():
            dn_copy(pos).wait_send()
        return carry
    lax.fori_loop(0, line, sent, 0)

    def sent_others(o):
        ss_copy(o, o).wait_send()
        q_copy(o, o).wait_send()
        a_copy(o, o).wait_send()
    others(sent_others)


def fused_device(
    n, stream, norm_gain, w_query, w_keyval, w_out, lengths, key_cache, value_cache,
    key_scales, value_scales,
):
    rows, width = stream.shape
    local_rows = lengths.shape[0]
    span = key_cache.shape[1]
    line = n // 4
    qcols = w_query.shape[1]
    tile = (qcols // HD + 1) * local_rows
    qrows = n // KVH * tile
    half = HD // 2
    freq = jnp.exp(jnp.arange(half, dtype=F32) * (-2.0 * math.log(rope_base) / HD))
    angle = lengths.astype(F32)[:, None] * freq
    cosine, sine = jnp.cos(angle), jnp.sin(angle)
    cosine = jnp.tile(jnp.concatenate([cosine, cosine], axis=1), (qrows // local_rows, 1))
    sine = jnp.tile(jnp.concatenate([-sine, sine], axis=1), (qrows // local_rows, 1))
    kfac = jnp.exp2(key_scales.astype(F32)).astype(BF16).astype(F32).reshape(-1)
    vfac = jnp.exp2(value_scales.astype(F32)).astype(BF16).astype(F32).reshape(-1)
    vmem = pl.BlockSpec(memory_space=pltpu.VMEM)
    smem = pl.BlockSpec(memory_space=pltpu.SMEM)
    hbm = pl.BlockSpec(memory_space=pl.ANY)
    kv_cols = w_keyval.shape[1]
    block = (rows, width)
    dma = pltpu.SemaphoreType.DMA
    return pl.pallas_call(
        functools.partial(fused_kernel, n, rows, width, local_rows, span),
        out_shape=jax.ShapeDtypeStruct(block, BF16),
        in_specs=[vmem] * 4 + [smem] * 3 + [hbm] * 5,
        out_specs=vmem,
        scratch_shapes=[
            pltpu.VMEM(w_query.shape, BF16),
            pltpu.VMEM((kv_cols, n * width), BF16),
            pltpu.VMEM(w_out.shape, BF16),
            pltpu.VMEM(key_cache.shape, BF16),
            pltpu.VMEM(value_cache.shape, BF16),
            pltpu.VMEM((n,) + block, BF16),
            pltpu.VMEM((8, 128), F32),
            pltpu.VMEM((n, 8, 128), F32),
            pltpu.VMEM((rows, qcols), F32),
            pltpu.VMEM((rows, kv_cols), F32),
            pltpu.VMEM((n, tile, HD), F32),
            pltpu.VMEM((n, tile, HD), BF16),
            pltpu.VMEM((n, tile, HD), BF16),
            pltpu.VMEM((n, tile, HD), BF16),
            pltpu.VMEM((n, tile, HD), BF16),
            pltpu.VMEM((rows, qcols), F32),
            pltpu.VMEM((2 * line,) + block, BF16),
            pltpu.VMEM((2 * line,) + block, BF16),
            pltpu.VMEM((line,) + block, BF16),
            pltpu.VMEM((line,) + block, BF16),
            pltpu.VMEM((line,) + block, BF16),
            pltpu.VMEM((line,) + block, BF16),
            pltpu.VMEM((line,) + block, BF16),
            pltpu.VMEM(block, F32),
            dma((n,)), dma((4,)), dma((3,)),
            dma((n,)), dma((line,)), dma((line,)), dma((line,)), dma((2 * line,)),
            dma((n,)), dma((n,)), dma((n,)), dma((n,)), dma((n,)), dma((n,)),
            dma((2 * line,)), dma((2 * line,)), dma((line,)), dma((line,)), dma((line,)),
            dma((line,)), dma((line,)),
        ],
        compiler_params=pltpu.CompilerParams(
            collective_id=0, has_side_effects=True, vmem_limit_bytes=52 * 2**20
        ),
        cost_estimate=pl.CostEstimate(
            flops=4 * rows * w_query.size, bytes_accessed=4 * w_query.size, transcendentals=0
        ),
    )(
        stream, norm_gain.reshape(1, -1), cosine, sine, lengths, kfac, vfac,
        w_query, w_keyval.T, w_out, key_cache, value_cache,
    )


def per_device(n, *args):
    stream, _, w_query, w_keyval, _, lengths, key_cache, *_ = args
    rows, width = stream.shape
    local_rows = lengths.shape[0]
    qcols, kv_cols = w_query.shape[1], w_keyval.shape[1]
    tiles = (
        n % 4 == 0 and n % KVH == 0 and width % 128 == 0 and qcols % HD == 0
        and HD % kv_cols == 0 and rows % 16 == 0 and rows <= 128
        and (qcols // HD + 1) * local_rows % 16 == 0
        and key_cache.shape[1] // 128 == args[8].shape[1]
    )
    return fused_device(n, *args) if tiles else plain_device(*args)


def solution(mesh):
    return jax.shard_map(
        functools.partial(per_device, mesh.shape["out"]),
        mesh=mesh,
        in_specs=(
            P("groups", "out"),
            P(),
            P(None, "out"),
            P(None, "out"),
            P("out", None),
            P(("groups", "out")),
            P(("groups", "out"), None, None),
            P(("groups", "out"), None, None),
            P(("groups", "out"), None, None),
            P(("groups", "out"), None, None),
        ),
        out_specs=P("groups", "out"),
        check_vma=False,
    )
```

```python
import functools
import math

import jax
import jax.numpy as jnp
from jax import lax
from jax.experimental import pallas as pl
from jax.experimental.pallas import tpu as pltpu
from jax.sharding import PartitionSpec as P

HQ = 48
KVH = 4
HD = 128


rope_base = 1000000.0
norm_eps = 1e-05


def rotate(vec, position):
    half = vec.shape[-1] // 2
    index = jnp.arange(half, dtype=jnp.float32)
    freq = jnp.exp(index * (-2.0 * math.log(rope_base) / vec.shape[-1]))
    angle = position * freq
    cosine = jnp.cos(angle)
    sine = jnp.sin(angle)
    first = vec[..., :half]
    second = vec[..., half:]
    return jnp.concatenate(
        [first * cosine - second * sine, second * cosine + first * sine], axis=-1
    )


def dequant(cache, scales):
    rows, span, width = cache.shape
    blocks = scales.shape[1]
    factor = jnp.exp2(scales.astype(jnp.float32)).astype(jnp.bfloat16)
    shaped = cache.reshape(rows, blocks, span // blocks, KVH, width // KVH)
    return (shaped * factor[:, :, None, :, None]).reshape(rows, span, KVH, width // KVH)


def plain_device(
    stream,
    norm_gain,
    w_query,
    w_keyval,
    w_out,
    lengths,
    key_cache,
    value_cache,
    key_scales,
    value_scales,
):
    local_rows = lengths.shape[0]
    xf = stream.astype(jnp.float32)
    whole = lax.all_gather(stream, "out", axis=1, tiled=True).astype(jnp.float32)
    meansq = jnp.mean(whole * whole, axis=-1, keepdims=True)
    normed = (whole * lax.rsqrt(meansq + norm_eps) * norm_gain).astype(jnp.bfloat16)
    q_local = jnp.dot(normed, w_query, preferred_element_type=jnp.float32).astype(jnp.bfloat16)
    kv_local = jnp.dot(normed, w_keyval, preferred_element_type=jnp.float32).astype(jnp.bfloat16)
    q_rows, kv_rows = (
        lax.all_to_all(q_local, "out", split_axis=0, concat_axis=1, tiled=True),
        lax.all_to_all(kv_local, "out", split_axis=0, concat_axis=1, tiled=True),
    )
    position = lengths.astype(jnp.float32)[:, None, None]
    rotated = rotate(q_rows.astype(jnp.float32).reshape(local_rows, HQ, HD), position).astype(
        jnp.bfloat16
    )
    rotated = rotated.reshape(local_rows, KVH, HQ // KVH, HD)
    new_key = rotate(
        kv_rows[:, : KVH * HD].astype(jnp.float32).reshape(local_rows, KVH, HD), position
    ).astype(jnp.bfloat16)
    new_value = kv_rows[:, KVH * HD :].reshape(local_rows, KVH, HD)
    factor = HD ** (-0.5)
    own = jnp.einsum("rkgd,rkd->rkg", rotated, new_key, preferred_element_type=jnp.float32) * factor
    span = key_cache.shape[1]
    scores = (
        jnp.einsum(
            "rkgd,rjkd->rkgj",
            rotated,
            dequant(key_cache, key_scales),
            preferred_element_type=jnp.float32,
        )
        * factor
    )
    valid = jnp.arange(span, dtype=jnp.int32)[None, :] < lengths[:, None]
    scores = jnp.where(valid[:, None, None, :], scores, -jnp.inf)
    top = jnp.maximum(jnp.max(scores, axis=-1), own)
    weights = jnp.exp(scores - top[..., None])
    own_weight = jnp.exp(own - top)
    total = jnp.sum(weights, axis=-1) + own_weight
    own_rounded = lax.optimization_barrier(own_weight.astype(jnp.bfloat16)).astype(jnp.float32)
    summed = jnp.einsum(
        "rkgj,rjkd->rkgd",
        weights.astype(jnp.bfloat16),
        dequant(value_cache, value_scales),
        preferred_element_type=jnp.float32,
    )
    summed = summed + own_rounded[..., None] * new_value.astype(jnp.float32)[:, :, None, :]
    attended = (summed / total[..., None]).astype(jnp.bfloat16).reshape(local_rows, HQ * HD)
    heads = lax.all_to_all(attended, "out", split_axis=1, concat_axis=0, tiled=True)
    partial_terms = jnp.dot(heads, w_out, preferred_element_type=jnp.float32)
    projected = lax.psum_scatter(partial_terms, "out", scatter_dimension=1, tiled=True)
    return (xf + projected).astype(jnp.bfloat16)


MESH = pl.DeviceIdType.MESH
F32 = jnp.float32
BF16 = jnp.bfloat16
CONTRACT_LAST = (((1,), (1,)), ((), ()))


def fused_kernel(
    n, rows, width, local_rows, span,
    len_ref, ks_ref, vs_ref,
    x_hbm, gain_hbm, wq_hbm, wkv_hbm, wo_hbm, kc_hbm, vc_hbm,
    out_ref,
    x_ref, gain_ref, cos_ref, sin_ref, kfac, vfac, wq, wkv, wo, kc, vc, xbuf, ssend, sbuf, accq, acckv, pk, qsend, qbuf, asend, abuf, heads,
    core_sb, core_rb, y_sb, y_rb, z_sb, up_rb, dn_rb, heads_sum,
    wq_sem, wo_sem, w_sem,
    ag_recv, ag_up, ag_dn, ag_y, ag_core,
    ss_send, ss_recv, q_send, q_recv, a_send, a_recv,
    core_send, core_recv, y_send, y_recv, z_send, up_recv, dn_recv,
):
    line = n // 4
    qcols = wq.shape[1]
    own_heads = qcols // HD
    tile = qbuf.shape[1]
    per_head = n // KVH
    qrows = per_head * tile
    me = lax.axis_index("out")
    grp = lax.axis_index("groups")
    a = me // 4
    b = (me // 2) % 2
    c = me % 2

    def at(pos, bb, cc):
        return (pos * 2 + bb) * 2 + cc

    up, down = at(a + 1, b, c), at(a - 1, b, c)
    ypeer, cpeer = at(a, 1 - b, c), at(a, b, 1 - c)
    low, high = a, line - 1 - a
    least = jnp.minimum(low, high)

    def ranked(m):
        d = (m + 1) // 2
        near = jnp.where(m % 2 == 1, a - d, a + d)
        far = jnp.where(high > low, a + (m - least), a - (m - least))
        return jnp.where(m <= 2 * least, near, far)

    def remote(src, dst, ssem, rsem, to):
        return pltpu.make_async_remote_copy(
            src_ref=src, dst_ref=dst, send_sem=ssem, recv_sem=rsem,
            device_id=(grp, to), device_id_type=MESH,
        )

    def wq_copy(i):
        at_rows = pl.ds(pl.multiple_of(i * width, width), width)
        return pltpu.make_async_copy(wq_hbm.at[at_rows], wq.at[at_rows], wq_sem.at[i])

    wo_parts = wo_sem.shape[0]
    wo_rows = wo.shape[0] // wo_parts

    def wo_copy(i):
        at_rows = pl.ds(i * wo_rows, wo_rows)
        return pltpu.make_async_copy(wo_hbm.at[at_rows], wo.at[at_rows], wo_sem.at[i])

    wkv_copy = pltpu.make_async_copy(wkv_hbm, wkv, w_sem.at[0])
    kc_copy = pltpu.make_async_copy(kc_hbm, kc, w_sem.at[1])
    vc_copy = pltpu.make_async_copy(vc_hbm, vc, w_sem.at[2])

    x_copy = pltpu.make_async_copy(x_hbm, x_ref, w_sem.at[3])
    gain_copy = pltpu.make_async_copy(gain_hbm, gain_ref, w_sem.at[4])
    x_copy.start()
    gain_copy.start()

    barrier = pltpu.get_barrier_semaphore()

    def others(body):
        def step(i, carry):
            body(lax.rem(me + i, n))
            return carry
        lax.fori_loop(1, n, step, 0)

    others(lambda o: pl.semaphore_signal(barrier, inc=1, device_id=(grp, o), device_id_type=MESH))

    wkv_copy.start()

    def start_wq(i, carry):
        wq_copy(lax.rem(me + i, n)).start()
        return carry
    lax.fori_loop(0, n, start_wq, 0)
    kc_copy.start()
    vc_copy.start()
    for i in range(wo_parts):
        wo_copy(i).start()

    x_copy.wait()
    xbuf[me] = x_ref[...]
    xf = x_ref[...].astype(F32)
    square = jnp.sum(xf * xf, axis=1, keepdims=True)
    spread = jnp.transpose(jnp.broadcast_to(square, (rows, 128)))
    ssend[...] = jnp.zeros_like(ssend)
    ssend[:, 0:rows] = spread[0:8, :]
    sbuf[me] = ssend[...]
    accq[...] = jnp.zeros_like(accq)
    acckv[...] = jnp.zeros_like(acckv)

    ridx = lax.broadcasted_iota(jnp.int32, (qrows, 128), 0) % local_rows
    pick = lax.broadcasted_iota(jnp.int32, (qrows, tile), 0) % local_rows
    pick = pick + own_heads * local_rows == lax.broadcasted_iota(jnp.int32, (qrows, tile), 1)
    pick = pick.astype(F32).astype(BF16)
    blocks = span // 128
    few = lax.broadcasted_iota(jnp.int32, (8, 128), 0) % local_rows
    lane8 = lax.broadcasted_iota(jnp.int32, (8, 128), 1)

    def by_row(values):
        res = jnp.full((8, 128), values[0])
        for r in range(1, local_rows):
            res = jnp.where(few == r, values[r], res)
        return res

    def tall(v):
        return jnp.concatenate([v] * (qrows // 8), axis=0)

    limit8 = by_row([len_ref[r] for r in range(local_rows)])
    freq = jnp.exp((lane8 % (HD // 2)).astype(F32) * (-2.0 * math.log(rope_base) / HD))
    angle = limit8.astype(F32) * freq
    cos_ref[...] = jnp.cos(angle)
    sin_ref[...] = jnp.where(lane8 < HD // 2, -1.0, 1.0) * jnp.sin(angle)
    for k in range(KVH):
        for u in range(blocks):
            for ref, table in ((ks_ref, kfac), (vs_ref, vfac)):
                power = by_row([ref[r, u, k] for r in range(local_rows)]).astype(F32)
                table[k * blocks + u] = jnp.exp2(power).astype(BF16).astype(F32)

    pl.semaphore_wait(barrier, n - 1)

    half_rows = rows // 2

    def ag_copy(block, h, ssem, to):
        part = xbuf.at[block, pl.ds(h * half_rows, half_rows)]
        return remote(part, part, ssem, ag_recv.at[2 * block + h], to)

    def ag_wait(block, h):
        ag_copy(block, h, ag_core.at[0], cpeer).wait_recv()

    def spread_line(pos, h):
        block = at(pos, b, c)

        @pl.when((pos <= a) & (a < line - 1))
        def _():
            ag_copy(block, h, ag_up.at[2 * pos + h], up).start()

        @pl.when((pos >= a) & (a > 0))
        def _():
            ag_copy(block, h, ag_dn.at[2 * pos + h], down).start()

        ag_copy(block, h, ag_y.at[2 * pos + h], ypeer).start()
        ag_copy(block, h, ag_core.at[2 * pos + h], cpeer).start()

    def ss_copy(o, slot):
        return remote(ssend, sbuf.at[slot], ss_send.at[o], ss_recv.at[slot], o)

    others(lambda o: ss_copy(o, me).start())
    for h in range(2):
        spread_line(a, h)
    others(lambda o: ss_copy(o, o).wait_recv())
    total_sq = jnp.sum(sbuf[...], axis=0)[0:1, :]
    column = jnp.transpose(jnp.broadcast_to(total_sq, (128, 128)))[0:rows, 0:1]
    scale = lax.rsqrt(column * (1.0 / (n * width)) + norm_eps)
    gain_copy.wait()
    wkv_copy.wait()

    def project(block):
        wq_copy(block).wait()
        start = pl.multiple_of(block * width, width)
        normed = (xbuf[block].astype(F32) * scale * gain_ref[:, pl.ds(start, width)]).astype(BF16)
        accq[...] += jnp.dot(normed, wq[pl.ds(start, width), :], preferred_element_type=F32)
        acckv[...] += lax.dot_general(
            normed, wkv[:, pl.ds(start, width)], CONTRACT_LAST, preferred_element_type=F32
        )

    def take_line(m, h):
        @pl.when(m < line)
        def _():
            pos = ranked(m)
            ag_wait(at(pos, b, c), h)
            spread_line(pos, h)

    def take_pair(m, h):
        pos = ranked(m)
        block = at(pos, 1 - b, c)
        ag_wait(block, h)
        ag_copy(block, h, ag_core.at[2 * (line + pos) + h], cpeer).start()

    project(me)

    def gather_step(m, carry):
        take_line(m, 0)
        take_pair(m - 1, 0)
        cblock = at(ranked(m - 1), b, 1 - c)
        for h in range(2):
            ag_wait(cblock, h)
        project(cblock)
        take_line(m, 1)
        take_pair(m - 1, 1)
        project(at(ranked(m - 1), 1 - b, c))

        @pl.when(m < line)
        def _():
            project(at(ranked(m), b, c))

        @pl.when(m > 1)
        def _():
            block = at(ranked(m - 2), 1 - b, 1 - c)
            for h in range(2):
                ag_wait(block, h)
            project(block)
        return carry
    lax.fori_loop(1, line + 1, gather_step, 0)
    last = at(ranked(line - 1), 1 - b, 1 - c)
    for h in range(2):
        ag_wait(last, h)
    project(last)

    kv_cols = wkv.shape[0]
    pk[...] = jnp.zeros_like(pk)
    q_all = accq[...]
    kv_all = acckv[...]
    for j in range(n):
        mine = slice(j * local_rows, (j + 1) * local_rows)
        for g in range(own_heads):
            pk[j, g * local_rows:(g + 1) * local_rows, :] = q_all[mine, g * HD:(g + 1) * HD]
        pk[j, own_heads * local_rows:tile, 0:kv_cols] = kv_all[mine, :]
    qsend[...] = pk[...].astype(BF16)

    def q_copy(o, slot):
        return remote(qsend.at[o], qbuf.at[slot], q_send.at[o], q_recv.at[slot], o)

    others(lambda o: q_copy(o, me).start())
    qbuf[me] = qsend[me]

    limit = tall(limit8)
    lane = lax.broadcasted_iota(jnp.int32, (qrows, 128), 1)
    cosine, sine = tall(cos_ref[...]), tall(sin_ref[...])

    def rotated(v):
        return (v * cosine + pltpu.roll(v, HD // 2, 1) * sine).astype(BF16)

    kc_copy.wait()
    vc_copy.wait()
    others(lambda o: q_copy(o, o).wait_recv())

    pieces = HD // kv_cols
    factor = HD ** (-0.5)

    def new_head(first):
        res = None
        for p in range(pieces):
            part = jnp.dot(pick, qbuf[first + p], preferred_element_type=F32)
            part = part if p == 0 else pltpu.roll(part, p * kv_cols, 1)
            res = part if res is None else res + part
        return res

    for k in range(KVH):
        at_k = slice(k * HD, (k + 1) * HD)
        query = rotated(qbuf[k * per_head:(k + 1) * per_head].astype(F32).reshape(qrows, HD))
        new_key = rotated(new_head(k * pieces)).astype(F32)
        new_value = new_head((KVH + k) * pieces)
        own = jnp.sum(query.astype(F32) * new_key, axis=1, keepdims=True) * factor
        score = None
        for r in range(local_rows):
            one = lax.dot_general(query, kc[r, :, at_k], CONTRACT_LAST, preferred_element_type=F32)
            cut = [one[:, 128 * u:128 * (u + 1)] for u in range(blocks)]
            score = cut if r == 0 else [jnp.where(ridx == r, x, y) for x, y in zip(cut, score)]
        top = own
        for u in range(blocks):
            scales = tall(kfac[k * blocks + u])
            score[u] = jnp.where(lane + 128 * u < limit, score[u] * scales * factor, -jnp.inf)
            top = jnp.maximum(top, jnp.max(score[u], axis=1, keepdims=True))
        own_weight = jnp.exp(own - top)
        total = own_weight
        weights = []
        for u in range(blocks):
            weight = jnp.exp(score[u] - top)
            total = total + jnp.sum(weight, axis=1, keepdims=True)
            scales = tall(vfac[k * blocks + u])
            weights.append((weight.astype(BF16).astype(F32) * scales).astype(BF16))
        weights = jnp.concatenate(weights, axis=1)
        summed = None
        for r in range(local_rows):
            one = jnp.dot(weights, vc[r, :, at_k], preferred_element_type=F32)
            summed = one if r == 0 else jnp.where(ridx == r, one, summed)
        summed = summed + own_weight.astype(BF16).astype(F32) * new_value
        result = (summed / total).astype(BF16)
        for s in range(per_head):
            asend[k * per_head + s] = result[s * tile:(s + 1) * tile, :]

    def a_copy(o, slot):
        return remote(asend.at[o], abuf.at[slot], a_send.at[o], a_recv.at[slot], o)

    others(lambda o: a_copy(o, me).start())
    abuf[me] = asend[me]
    for i in range(wo_parts):
        wo_copy(i).wait()
    others(lambda o: a_copy(o, o).wait_recv())
    pk[...] = abuf[...].astype(F32)
    for j in range(n):
        for g in range(own_heads):
            heads[j * local_rows:(j + 1) * local_rows, g * HD:(g + 1) * HD] = (
                pk[j, g * local_rows:(g + 1) * local_rows, :]
            )
    attended = heads[...].astype(BF16)

    def partial(block):
        start = pl.multiple_of(block * width, width)
        return jnp.dot(attended, wo[:, pl.ds(start, width)], preferred_element_type=F32)

    def core_copy(slot):
        return remote(core_sb.at[slot], core_rb.at[slot], core_send.at[slot], core_recv.at[slot], cpeer)

    def y_copy(pos):
        return remote(y_sb.at[pos], y_rb.at[pos], y_send.at[pos], y_recv.at[pos], ypeer)

    def up_copy(pos):
        return remote(z_sb.at[pos], up_rb.at[pos], z_send.at[pos], up_recv.at[pos], up)

    def dn_copy(pos):
        return remote(z_sb.at[pos], dn_rb.at[pos], z_send.at[pos], dn_recv.at[pos], down)

    def loop_far(body):
        def step(m, carry):
            body(ranked(line - 1 - m))
            return carry
        lax.fori_loop(0, line, step, 0)

    def to_core_far(pos):
        core_sb[line + pos] = partial(at(pos, 1 - b, 1 - c)).astype(BF16)
        core_copy(line + pos).start()

    def to_pair(pos):
        term = partial(at(pos, 1 - b, c))
        core_copy(line + pos).wait_recv()
        y_sb[pos] = (term + core_rb[line + pos].astype(F32)).astype(BF16)
        y_copy(pos).start()

    def to_core_near(pos):
        core_sb[pos] = partial(at(pos, b, 1 - c)).astype(BF16)
        core_copy(pos).start()

    def to_line(pos):
        term = partial(at(pos, b, c))
        core_copy(pos).wait_recv()
        term = term + core_rb[pos].astype(F32)
        y_copy(pos).wait_recv()
        term = term + y_rb[pos].astype(F32)
        heads_sum[...] = term

        @pl.when((pos >= a) & (a > 0))
        def _():
            up_copy(pos).wait_recv()
            heads_sum[...] += up_rb[pos].astype(F32)

        @pl.when((pos <= a) & (a < line - 1))
        def _():
            dn_copy(pos).wait_recv()
            heads_sum[...] += dn_rb[pos].astype(F32)

        @pl.when(pos > a)
        def _():
            z_sb[pos] = heads_sum[...].astype(BF16)
            up_copy(pos).start()

        @pl.when(pos < a)
        def _():
            z_sb[pos] = heads_sum[...].astype(BF16)
            dn_copy(pos).start()

        @pl.when(pos == a)
        def _():
            out_ref[...] = (x_ref[...].astype(F32) + heads_sum[...]).astype(BF16)

    def far(m):
        return ranked(line - 1 - m)

    to_core_far(far(0))

    def pair_step(m, carry):
        @pl.when(m < line - 1)
        def _():
            to_core_far(far(m + 1))
        to_pair(far(m))
        return carry
    lax.fori_loop(0, line, pair_step, 0)
    loop_far(to_core_near)
    loop_far(to_line)

    def sent_gather(i, carry):
        pos, h = i // 2, i % 2
        block = at(pos, b, c)

        @pl.when((pos <= a) & (a < line - 1))
        def _():
            ag_copy(block, h, ag_up.at[2 * pos + h], up).wait_send()

        @pl.when((pos >= a) & (a > 0))
        def _():
            ag_copy(block, h, ag_dn.at[2 * pos + h], down).wait_send()

        ag_copy(block, h, ag_y.at[2 * pos + h], ypeer).wait_send()
        ag_copy(block, h, ag_core.at[2 * pos + h], cpeer).wait_send()
        ag_copy(at(pos, 1 - b, c), h, ag_core.at[2 * (line + pos) + h], cpeer).wait_send()
        return carry
    lax.fori_loop(0, 2 * line, sent_gather, 0)

    def sent(pos, carry):
        core_copy(pos).wait_send()
        core_copy(line + pos).wait_send()
        y_copy(pos).wait_send()

        @pl.when(pos > a)
        def _():
            up_copy(pos).wait_send()

        @pl.when(pos < a)
        def _():
            dn_copy(pos).wait_send()
        return carry
    lax.fori_loop(0, line, sent, 0)

    def sent_others(o):
        ss_copy(o, o).wait_send()
        q_copy(o, o).wait_send()
        a_copy(o, o).wait_send()
    others(sent_others)


def fused_device(
    n, stream, norm_gain, w_query, w_keyval, w_out, lengths, key_cache, value_cache,
    key_scales, value_scales,
):
    rows, width = stream.shape
    local_rows = lengths.shape[0]
    span = key_cache.shape[1]
    line = n // 4
    qcols = w_query.shape[1]
    tile = (qcols // HD + 1) * local_rows
    vmem = pl.BlockSpec(memory_space=pltpu.VMEM)
    smem = pl.BlockSpec(memory_space=pltpu.SMEM)
    hbm = pl.BlockSpec(memory_space=pl.ANY)
    kv_cols = w_keyval.shape[1]
    block = (rows, width)
    dma = pltpu.SemaphoreType.DMA
    return pl.pallas_call(
        functools.partial(fused_kernel, n, rows, width, local_rows, span),
        out_shape=jax.ShapeDtypeStruct(block, BF16),
        in_specs=[smem] * 3 + [hbm] * 7,
        out_specs=vmem,
        scratch_shapes=[
            pltpu.VMEM(block, BF16),
            pltpu.VMEM((1, n * width), F32),
            pltpu.VMEM((8, HD), F32),
            pltpu.VMEM((8, HD), F32),
            pltpu.VMEM((KVH * (span // 128), 8, 128), F32),
            pltpu.VMEM((KVH * (span // 128), 8, 128), F32),
            pltpu.VMEM(w_query.shape, BF16),
            pltpu.VMEM((kv_cols, n * width), BF16),
            pltpu.VMEM(w_out.shape, BF16),
            pltpu.VMEM(key_cache.shape, BF16),
            pltpu.VMEM(value_cache.shape, BF16),
            pltpu.VMEM((n,) + block, BF16),
            pltpu.VMEM((8, 128), F32),
            pltpu.VMEM((n, 8, 128), F32),
            pltpu.VMEM((rows, qcols), F32),
            pltpu.VMEM((rows, kv_cols), F32),
            pltpu.VMEM((n, tile, HD), F32),
            pltpu.VMEM((n, tile, HD), BF16),
            pltpu.VMEM((n, tile, HD), BF16),
            pltpu.VMEM((n, tile, HD), BF16),
            pltpu.VMEM((n, tile, HD), BF16),
            pltpu.VMEM((rows, qcols), F32),
            pltpu.VMEM((2 * line,) + block, BF16),
            pltpu.VMEM((2 * line,) + block, BF16),
            pltpu.VMEM((line,) + block, BF16),
            pltpu.VMEM((line,) + block, BF16),
            pltpu.VMEM((line,) + block, BF16),
            pltpu.VMEM((line,) + block, BF16),
            pltpu.VMEM((line,) + block, BF16),
            pltpu.VMEM(block, F32),
            dma((n,)), dma((4,)), dma((5,)),
            dma((2 * n,)), dma((2 * line,)), dma((2 * line,)), dma((2 * line,)), dma((4 * line,)),
            dma((n,)), dma((n,)), dma((n,)), dma((n,)), dma((n,)), dma((n,)),
            dma((2 * line,)), dma((2 * line,)), dma((line,)), dma((line,)), dma((line,)),
            dma((line,)), dma((line,)),
        ],
        compiler_params=pltpu.CompilerParams(
            collective_id=0, has_side_effects=True, vmem_limit_bytes=62 * 2**20
        ),
        cost_estimate=pl.CostEstimate(
            flops=4 * rows * w_query.size, bytes_accessed=4 * w_query.size, transcendentals=0
        ),
    )(
        lengths, key_scales, value_scales, stream, norm_gain.reshape(1, -1),
        w_query, w_keyval.T, w_out, key_cache, value_cache,
    )


def per_device(n, *args):
    stream, _, w_query, w_keyval, _, lengths, key_cache, *_ = args
    rows, width = stream.shape
    local_rows = lengths.shape[0]
    qcols, kv_cols = w_query.shape[1], w_keyval.shape[1]
    tiles = (
        n % 4 == 0 and n % KVH == 0 and width % 128 == 0 and qcols % HD == 0
        and HD % kv_cols == 0 and rows % 32 == 0 and rows <= 128
        and 8 % local_rows == 0
        and (qcols // HD + 1) * local_rows % 16 == 0
        and key_cache.shape[1] // 128 == args[8].shape[1]
    )
    return fused_device(n, *args) if tiles else plain_device(*args)


def solution(mesh):
    return jax.shard_map(
        functools.partial(per_device, mesh.shape["out"]),
        mesh=mesh,
        in_specs=(
            P("groups", "out"),
            P(),
            P(None, "out"),
            P(None, "out"),
            P("out", None),
            P(("groups", "out")),
            P(("groups", "out"), None, None),
            P(("groups", "out"), None, None),
            P(("groups", "out"), None, None),
            P(("groups", "out"), None, None),
        ),
        out_specs=P("groups", "out"),
        check_vma=False,
    )
```

```python
import functools
import math

import jax
import jax.numpy as jnp
from jax import lax
from jax.experimental import pallas as pl
from jax.experimental.pallas import tpu as pltpu
from jax.sharding import PartitionSpec as P

HQ = 48
KVH = 4
HD = 128


rope_base = 1000000.0
norm_eps = 1e-05


def rotate(vec, position):
    half = vec.shape[-1] // 2
    index = jnp.arange(half, dtype=jnp.float32)
    freq = jnp.exp(index * (-2.0 * math.log(rope_base) / vec.shape[-1]))
    angle = position * freq
    cosine = jnp.cos(angle)
    sine = jnp.sin(angle)
    first = vec[..., :half]
    second = vec[..., half:]
    return jnp.concatenate(
        [first * cosine - second * sine, second * cosine + first * sine], axis=-1
    )


def dequant(cache, scales):
    rows, span, width = cache.shape
    blocks = scales.shape[1]
    factor = jnp.exp2(scales.astype(jnp.float32)).astype(jnp.bfloat16)
    shaped = cache.reshape(rows, blocks, span // blocks, KVH, width // KVH)
    return (shaped * factor[:, :, None, :, None]).reshape(rows, span, KVH, width // KVH)


def plain_device(
    stream,
    norm_gain,
    w_query,
    w_keyval,
    w_out,
    lengths,
    key_cache,
    value_cache,
    key_scales,
    value_scales,
):
    local_rows = lengths.shape[0]
    xf = stream.astype(jnp.float32)
    whole = lax.all_gather(stream, "out", axis=1, tiled=True).astype(jnp.float32)
    meansq = jnp.mean(whole * whole, axis=-1, keepdims=True)
    normed = (whole * lax.rsqrt(meansq + norm_eps) * norm_gain).astype(jnp.bfloat16)
    q_local = jnp.dot(normed, w_query, preferred_element_type=jnp.float32).astype(jnp.bfloat16)
    kv_local = jnp.dot(normed, w_keyval, preferred_element_type=jnp.float32).astype(jnp.bfloat16)
    q_rows, kv_rows = (
        lax.all_to_all(q_local, "out", split_axis=0, concat_axis=1, tiled=True),
        lax.all_to_all(kv_local, "out", split_axis=0, concat_axis=1, tiled=True),
    )
    position = lengths.astype(jnp.float32)[:, None, None]
    rotated = rotate(q_rows.astype(jnp.float32).reshape(local_rows, HQ, HD), position).astype(
        jnp.bfloat16
    )
    rotated = rotated.reshape(local_rows, KVH, HQ // KVH, HD)
    new_key = rotate(
        kv_rows[:, : KVH * HD].astype(jnp.float32).reshape(local_rows, KVH, HD), position
    ).astype(jnp.bfloat16)
    new_value = kv_rows[:, KVH * HD :].reshape(local_rows, KVH, HD)
    factor = HD ** (-0.5)
    own = jnp.einsum("rkgd,rkd->rkg", rotated, new_key, preferred_element_type=jnp.float32) * factor
    span = key_cache.shape[1]
    scores = (
        jnp.einsum(
            "rkgd,rjkd->rkgj",
            rotated,
            dequant(key_cache, key_scales),
            preferred_element_type=jnp.float32,
        )
        * factor
    )
    valid = jnp.arange(span, dtype=jnp.int32)[None, :] < lengths[:, None]
    scores = jnp.where(valid[:, None, None, :], scores, -jnp.inf)
    top = jnp.maximum(jnp.max(scores, axis=-1), own)
    weights = jnp.exp(scores - top[..., None])
    own_weight = jnp.exp(own - top)
    total = jnp.sum(weights, axis=-1) + own_weight
    own_rounded = lax.optimization_barrier(own_weight.astype(jnp.bfloat16)).astype(jnp.float32)
    summed = jnp.einsum(
        "rkgj,rjkd->rkgd",
        weights.astype(jnp.bfloat16),
        dequant(value_cache, value_scales),
        preferred_element_type=jnp.float32,
    )
    summed = summed + own_rounded[..., None] * new_value.astype(jnp.float32)[:, :, None, :]
    attended = (summed / total[..., None]).astype(jnp.bfloat16).reshape(local_rows, HQ * HD)
    heads = lax.all_to_all(attended, "out", split_axis=1, concat_axis=0, tiled=True)
    partial_terms = jnp.dot(heads, w_out, preferred_element_type=jnp.float32)
    projected = lax.psum_scatter(partial_terms, "out", scatter_dimension=1, tiled=True)
    return (xf + projected).astype(jnp.bfloat16)


MESH = pl.DeviceIdType.MESH
F32 = jnp.float32
BF16 = jnp.bfloat16
CONTRACT_LAST = (((1,), (1,)), ((), ()))


def fused_kernel(
    n, rows, width, local_rows, span,
    len_ref, ks_ref, vs_ref,
    x_hbm, gain_hbm, wq_hbm, wkv_hbm, wo_hbm, kc_hbm, vc_hbm,
    out_ref,
    x_ref, gain_ref, cos_ref, sin_ref, kfac, vfac, wq, wkv, wo, kc, vc, xbuf, ssend, sbuf, accq, acckv, pk, qsend, qbuf, asend, abuf, heads,
    core_sb, core_rb, y_sb, y_rb, z_sb, up_rb, dn_rb, heads_sum,
    wq_sem, wo_sem, w_sem,
    ag_recv, ag_up, ag_dn, ag_y, ag_core,
    ss_send, ss_recv, q_send, q_recv, a_send, a_recv,
    core_send, core_recv, y_send, y_recv, z_send, up_recv, dn_recv,
):
    line = n // 4
    qcols = wq.shape[1]
    own_heads = qcols // HD
    tile = qbuf.shape[1]
    per_head = n // KVH
    qrows = per_head * tile
    me = lax.axis_index("out")
    grp = lax.axis_index("groups")
    a = me // 4
    b = (me // 2) % 2
    c = me % 2

    def at(pos, bb, cc):
        return (pos * 2 + bb) * 2 + cc

    up, down = at(a + 1, b, c), at(a - 1, b, c)
    ypeer, cpeer = at(a, 1 - b, c), at(a, b, 1 - c)
    low, high = a, line - 1 - a
    least = jnp.minimum(low, high)

    def ranked(m):
        d = (m + 1) // 2
        near = jnp.where(m % 2 == 1, a - d, a + d)
        far = jnp.where(high > low, a + (m - least), a - (m - least))
        return jnp.where(m <= 2 * least, near, far)

    def remote(src, dst, ssem, rsem, to):
        return pltpu.make_async_remote_copy(
            src_ref=src, dst_ref=dst, send_sem=ssem, recv_sem=rsem,
            device_id=(grp, to), device_id_type=MESH,
        )

    def wq_copy(i):
        at_rows = pl.ds(pl.multiple_of(i * width, width), width)
        return pltpu.make_async_copy(wq_hbm.at[at_rows], wq.at[at_rows], wq_sem.at[i])

    wo_parts = wo_sem.shape[0]
    wo_rows = wo.shape[0] // wo_parts

    def wo_copy(i):
        at_rows = pl.ds(i * wo_rows, wo_rows)
        return pltpu.make_async_copy(wo_hbm.at[at_rows], wo.at[at_rows], wo_sem.at[i])

    wkv_copy = pltpu.make_async_copy(wkv_hbm, wkv, w_sem.at[0])
    kc_copy = pltpu.make_async_copy(kc_hbm, kc, w_sem.at[1])
    vc_copy = pltpu.make_async_copy(vc_hbm, vc, w_sem.at[2])

    x_copy = pltpu.make_async_copy(x_hbm, x_ref, w_sem.at[3])
    gain_copy = pltpu.make_async_copy(gain_hbm, gain_ref, w_sem.at[4])
    x_copy.start()
    gain_copy.start()

    barrier = pltpu.get_barrier_semaphore()

    def others(body):
        def step(i, carry):
            body(lax.rem(me + i, n))
            return carry
        lax.fori_loop(1, n, step, 0)

    others(lambda o: pl.semaphore_signal(barrier, inc=1, device_id=(grp, o), device_id_type=MESH))

    wkv_copy.start()

    def start_wq(m, carry):
        pos = ranked(m)
        for bb, cc in ((b, c), (b, 1 - c), (1 - b, c), (1 - b, 1 - c)):
            wq_copy(at(pos, bb, cc)).start()
        return carry
    lax.fori_loop(0, line, start_wq, 0)

    x_copy.wait()
    xbuf[me] = x_ref[...]
    xf = x_ref[...].astype(F32)
    square = jnp.sum(xf * xf, axis=1, keepdims=True)
    spread = jnp.transpose(jnp.broadcast_to(square, (rows, 128)))
    ssend[...] = jnp.zeros_like(ssend)
    ssend[:, 0:rows] = spread[0:8, :]
    sbuf[me] = ssend[...]
    accq[...] = jnp.zeros_like(accq)
    acckv[...] = jnp.zeros_like(acckv)

    pl.semaphore_wait(barrier, n - 1)

    half_rows = rows // 2

    def ag_copy(block, h, ssem, to):
        part = xbuf.at[block, pl.ds(h * half_rows, half_rows)]
        return remote(part, part, ssem, ag_recv.at[2 * block + h], to)

    def ag_wait(block, h):
        ag_copy(block, h, ag_core.at[0], cpeer).wait_recv()

    def spread_line(pos, h):
        block = at(pos, b, c)

        @pl.when((pos <= a) & (a < line - 1))
        def _():
            ag_copy(block, h, ag_up.at[2 * pos + h], up).start()

        @pl.when((pos >= a) & (a > 0))
        def _():
            ag_copy(block, h, ag_dn.at[2 * pos + h], down).start()

        ag_copy(block, h, ag_y.at[2 * pos + h], ypeer).start()
        ag_copy(block, h, ag_core.at[2 * pos + h], cpeer).start()

    def ss_copy(o, slot):
        return remote(ssend, sbuf.at[slot], ss_send.at[o], ss_recv.at[slot], o)

    others(lambda o: ss_copy(o, me).start())
    for h in range(2):
        spread_line(a, h)
    ridx = lax.broadcasted_iota(jnp.int32, (qrows, 128), 0) % local_rows
    pick = lax.broadcasted_iota(jnp.int32, (qrows, tile), 0) % local_rows
    pick = pick + own_heads * local_rows == lax.broadcasted_iota(jnp.int32, (qrows, tile), 1)
    pick = pick.astype(F32).astype(BF16)
    blocks = span // 128
    few = lax.broadcasted_iota(jnp.int32, (8, 128), 0) % local_rows
    lane8 = lax.broadcasted_iota(jnp.int32, (8, 128), 1)

    def by_row(values):
        res = jnp.full((8, 128), values[0])
        for r in range(1, local_rows):
            res = jnp.where(few == r, values[r], res)
        return res

    def tall(v):
        return jnp.concatenate([v] * (qrows // 8), axis=0)

    limit8 = by_row([len_ref[r] for r in range(local_rows)])
    freq = jnp.exp((lane8 % (HD // 2)).astype(F32) * (-2.0 * math.log(rope_base) / HD))
    angle = limit8.astype(F32) * freq
    cos_ref[...] = jnp.cos(angle)
    sin_ref[...] = jnp.where(lane8 < HD // 2, -1.0, 1.0) * jnp.sin(angle)
    for k in range(KVH):
        for u in range(blocks):
            for ref, table in ((ks_ref, kfac), (vs_ref, vfac)):
                power = by_row([ref[r, u, k] for r in range(local_rows)]).astype(F32)
                table[k * blocks + u] = jnp.exp2(power).astype(BF16).astype(F32)

    others(lambda o: ss_copy(o, o).wait_recv())
    total_sq = jnp.sum(sbuf[...], axis=0)[0:1, :]
    column = jnp.transpose(jnp.broadcast_to(total_sq, (128, 128)))[0:rows, 0:1]
    scale = lax.rsqrt(column * (1.0 / (n * width)) + norm_eps)
    gain_copy.wait()
    wkv_copy.wait()

    def project(block):
        wq_copy(block).wait()
        start = pl.multiple_of(block * width, width)
        normed = (xbuf[block].astype(F32) * scale * gain_ref[:, pl.ds(start, width)]).astype(BF16)
        accq[...] += jnp.dot(normed, wq[pl.ds(start, width), :], preferred_element_type=F32)
        acckv[...] += lax.dot_general(
            normed, wkv[:, pl.ds(start, width)], CONTRACT_LAST, preferred_element_type=F32
        )

    def take_line(m, h):
        @pl.when(m < line)
        def _():
            pos = ranked(m)
            ag_wait(at(pos, b, c), h)
            spread_line(pos, h)

    def take_pair(m, h):
        pos = ranked(m)
        block = at(pos, 1 - b, c)
        ag_wait(block, h)
        ag_copy(block, h, ag_core.at[2 * (line + pos) + h], cpeer).start()

    project(me)

    def gather_step(m, carry):
        take_line(m, 0)
        take_pair(m - 1, 0)
        cblock = at(ranked(m - 1), b, 1 - c)
        for h in range(2):
            ag_wait(cblock, h)
        project(cblock)
        take_line(m, 1)
        take_pair(m - 1, 1)
        project(at(ranked(m - 1), 1 - b, c))

        @pl.when(m < line)
        def _():
            project(at(ranked(m), b, c))

        @pl.when(m > 1)
        def _():
            block = at(ranked(m - 2), 1 - b, 1 - c)
            for h in range(2):
                ag_wait(block, h)
            project(block)

        @pl.when(m == 1)
        def _():
            kc_copy.start()
            vc_copy.start()
            for i in range(wo_parts):
                wo_copy(i).start()
        return carry
    lax.fori_loop(1, line + 1, gather_step, 0)
    last = at(ranked(line - 1), 1 - b, 1 - c)
    for h in range(2):
        ag_wait(last, h)
    project(last)

    kv_cols = wkv.shape[0]
    pk[...] = jnp.zeros_like(pk)
    q_all = accq[...]
    kv_all = acckv[...]
    for j in range(n):
        mine = slice(j * local_rows, (j + 1) * local_rows)
        for g in range(own_heads):
            pk[j, g * local_rows:(g + 1) * local_rows, :] = q_all[mine, g * HD:(g + 1) * HD]
        pk[j, own_heads * local_rows:tile, 0:kv_cols] = kv_all[mine, :]
    qsend[...] = pk[...].astype(BF16)

    def q_copy(o, slot):
        return remote(qsend.at[o], qbuf.at[slot], q_send.at[o], q_recv.at[slot], o)

    others(lambda o: q_copy(o, me).start())
    qbuf[me] = qsend[me]

    limit = tall(limit8)
    lane = lax.broadcasted_iota(jnp.int32, (qrows, 128), 1)
    cosine, sine = tall(cos_ref[...]), tall(sin_ref[...])

    def rotated(v):
        return (v * cosine + pltpu.roll(v, HD // 2, 1) * sine).astype(BF16)

    kc_copy.wait()
    vc_copy.wait()
    others(lambda o: q_copy(o, o).wait_recv())

    pieces = HD // kv_cols
    factor = HD ** (-0.5)

    def new_head(first):
        res = None
        for p in range(pieces):
            part = jnp.dot(pick, qbuf[first + p], preferred_element_type=F32)
            part = part if p == 0 else pltpu.roll(part, p * kv_cols, 1)
            res = part if res is None else res + part
        return res

    for k in range(KVH):
        at_k = slice(k * HD, (k + 1) * HD)
        query = rotated(qbuf[k * per_head:(k + 1) * per_head].astype(F32).reshape(qrows, HD))
        new_key = rotated(new_head(k * pieces)).astype(F32)
        new_value = new_head((KVH + k) * pieces)
        own = jnp.sum(query.astype(F32) * new_key, axis=1, keepdims=True) * factor
        score = None
        for r in range(local_rows):
            one = lax.dot_general(query, kc[r, :, at_k], CONTRACT_LAST, preferred_element_type=F32)
            cut = [one[:, 128 * u:128 * (u + 1)] for u in range(blocks)]
            score = cut if r == 0 else [jnp.where(ridx == r, x, y) for x, y in zip(cut, score)]
        highest = None
        for u in range(blocks):
            scales = tall(kfac[k * blocks + u])
            score[u] = jnp.where(lane + 128 * u < limit, score[u] * scales * factor, -jnp.inf)
            highest = score[u] if u == 0 else jnp.maximum(highest, score[u])
        top = jnp.maximum(own, jnp.max(highest, axis=1, keepdims=True))
        own_weight = jnp.exp(own - top)
        added = None
        weights = []
        for u in range(blocks):
            weight = jnp.exp(score[u] - top)
            added = weight if u == 0 else added + weight
            scales = tall(vfac[k * blocks + u])
            weights.append((weight.astype(BF16).astype(F32) * scales).astype(BF16))
        total = own_weight + jnp.sum(added, axis=1, keepdims=True)
        weights = jnp.concatenate(weights, axis=1)
        summed = None
        for r in range(local_rows):
            one = jnp.dot(weights, vc[r, :, at_k], preferred_element_type=F32)
            summed = one if r == 0 else jnp.where(ridx == r, one, summed)
        summed = summed + own_weight.astype(BF16).astype(F32) * new_value
        result = (summed / total).astype(BF16)
        for s in range(per_head):
            asend[k * per_head + s] = result[s * tile:(s + 1) * tile, :]

    def a_copy(o, slot):
        return remote(asend.at[o], abuf.at[slot], a_send.at[o], a_recv.at[slot], o)

    others(lambda o: a_copy(o, me).start())
    abuf[me] = asend[me]
    for i in range(wo_parts):
        wo_copy(i).wait()
    others(lambda o: a_copy(o, o).wait_recv())
    pk[...] = abuf[...].astype(F32)
    for j in range(n):
        for g in range(own_heads):
            heads[j * local_rows:(j + 1) * local_rows, g * HD:(g + 1) * HD] = (
                pk[j, g * local_rows:(g + 1) * local_rows, :]
            )
    attended = heads[...].astype(BF16)

    def partial(block):
        start = pl.multiple_of(block * width, width)
        return jnp.dot(attended, wo[:, pl.ds(start, width)], preferred_element_type=F32)

    def core_copy(slot):
        return remote(core_sb.at[slot], core_rb.at[slot], core_send.at[slot], core_recv.at[slot], cpeer)

    def half_of(ref, pos, h):
        return ref.at[pos, pl.ds(h * half_rows, half_rows)]

    def y_copy(pos, h):
        i = 2 * pos + h
        return remote(half_of(y_sb, pos, h), half_of(y_rb, pos, h), y_send.at[i], y_recv.at[i], ypeer)

    def up_copy(pos, h):
        i = 2 * pos + h
        return remote(half_of(z_sb, pos, h), half_of(up_rb, pos, h), z_send.at[i], up_recv.at[i], up)

    def dn_copy(pos, h):
        i = 2 * pos + h
        return remote(half_of(z_sb, pos, h), half_of(dn_rb, pos, h), z_send.at[i], dn_recv.at[i], down)

    def to_core_far(pos):
        core_sb[line + pos] = partial(at(pos, 1 - b, 1 - c)).astype(BF16)
        core_copy(line + pos).start()

    def to_pair(pos):
        term = partial(at(pos, 1 - b, c))
        core_copy(line + pos).wait_recv()
        y_sb[pos] = (term + core_rb[line + pos].astype(F32)).astype(BF16)
        for h in range(2):
            y_copy(pos, h).start()

    def to_core_near(pos):
        core_sb[pos] = partial(at(pos, b, 1 - c)).astype(BF16)
        core_copy(pos).start()

    def to_line(pos):
        term = partial(at(pos, b, c))
        core_copy(pos).wait_recv()
        heads_sum[...] = term + core_rb[pos].astype(F32)
        for h in range(2):
            part = pl.ds(h * half_rows, half_rows)
            y_copy(pos, h).wait_recv()
            heads_sum[part] += y_rb[pos, part].astype(F32)

            @pl.when((pos >= a) & (a > 0))
            def _():
                up_copy(pos, h).wait_recv()
                heads_sum[part] += up_rb[pos, part].astype(F32)

            @pl.when((pos <= a) & (a < line - 1))
            def _():
                dn_copy(pos, h).wait_recv()
                heads_sum[part] += dn_rb[pos, part].astype(F32)

            @pl.when(pos > a)
            def _():
                z_sb[pos, part] = heads_sum[part].astype(BF16)
                up_copy(pos, h).start()

            @pl.when(pos < a)
            def _():
                z_sb[pos, part] = heads_sum[part].astype(BF16)
                dn_copy(pos, h).start()

            @pl.when(pos == a)
            def _():
                out_ref[part] = (x_ref[part].astype(F32) + heads_sum[part]).astype(BF16)

    def far(m):
        return ranked(line - 1 - m)

    to_core_far(far(0))
    to_core_far(far(1))
    to_pair(far(0))
    to_core_near(far(0))

    def sum_step(m, carry):
        @pl.when(m + 2 < line)
        def _():
            to_core_far(far(m + 2))

        @pl.when(m + 1 < line)
        def _():
            to_pair(far(m + 1))
            to_core_near(far(m + 1))

        to_line(far(m))
        return carry
    lax.fori_loop(0, line, sum_step, 0)

    def sent_gather(i, carry):
        pos, h = i // 2, i % 2
        block = at(pos, b, c)

        @pl.when((pos <= a) & (a < line - 1))
        def _():
            ag_copy(block, h, ag_up.at[2 * pos + h], up).wait_send()

        @pl.when((pos >= a) & (a > 0))
        def _():
            ag_copy(block, h, ag_dn.at[2 * pos + h], down).wait_send()

        ag_copy(block, h, ag_y.at[2 * pos + h], ypeer).wait_send()
        ag_copy(block, h, ag_core.at[2 * pos + h], cpeer).wait_send()
        ag_copy(at(pos, 1 - b, c), h, ag_core.at[2 * (line + pos) + h], cpeer).wait_send()
        y_copy(pos, h).wait_send()

        @pl.when(pos > a)
        def _():
            up_copy(pos, h).wait_send()

        @pl.when(pos < a)
        def _():
            dn_copy(pos, h).wait_send()
        return carry
    lax.fori_loop(0, 2 * line, sent_gather, 0)

    def sent(pos, carry):
        core_copy(pos).wait_send()
        core_copy(line + pos).wait_send()
        return carry
    lax.fori_loop(0, line, sent, 0)

    def sent_others(o):
        ss_copy(o, o).wait_send()
        q_copy(o, o).wait_send()
        a_copy(o, o).wait_send()
    others(sent_others)


def fused_device(
    n, stream, norm_gain, w_query, w_keyval, w_out, lengths, key_cache, value_cache,
    key_scales, value_scales,
):
    rows, width = stream.shape
    local_rows = lengths.shape[0]
    span = key_cache.shape[1]
    line = n // 4
    qcols = w_query.shape[1]
    tile = (qcols // HD + 1) * local_rows
    vmem = pl.BlockSpec(memory_space=pltpu.VMEM)
    smem = pl.BlockSpec(memory_space=pltpu.SMEM)
    hbm = pl.BlockSpec(memory_space=pl.ANY)
    kv_cols = w_keyval.shape[1]
    block = (rows, width)
    dma = pltpu.SemaphoreType.DMA
    return pl.pallas_call(
        functools.partial(fused_kernel, n, rows, width, local_rows, span),
        out_shape=jax.ShapeDtypeStruct(block, BF16),
        in_specs=[smem] * 3 + [hbm] * 7,
        out_specs=vmem,
        scratch_shapes=[
            pltpu.VMEM(block, BF16),
            pltpu.VMEM((1, n * width), F32),
            pltpu.VMEM((8, HD), F32),
            pltpu.VMEM((8, HD), F32),
            pltpu.VMEM((KVH * (span // 128), 8, 128), F32),
            pltpu.VMEM((KVH * (span // 128), 8, 128), F32),
            pltpu.VMEM(w_query.shape, BF16),
            pltpu.VMEM((kv_cols, n * width), BF16),
            pltpu.VMEM(w_out.shape, BF16),
            pltpu.VMEM(key_cache.shape, BF16),
            pltpu.VMEM(value_cache.shape, BF16),
            pltpu.VMEM((n,) + block, BF16),
            pltpu.VMEM((8, 128), F32),
            pltpu.VMEM((n, 8, 128), F32),
            pltpu.VMEM((rows, qcols), F32),
            pltpu.VMEM((rows, kv_cols), F32),
            pltpu.VMEM((n, tile, HD), F32),
            pltpu.VMEM((n, tile, HD), BF16),
            pltpu.VMEM((n, tile, HD), BF16),
            pltpu.VMEM((n, tile, HD), BF16),
            pltpu.VMEM((n, tile, HD), BF16),
            pltpu.VMEM((rows, qcols), F32),
            pltpu.VMEM((2 * line,) + block, BF16),
            pltpu.VMEM((2 * line,) + block, BF16),
            pltpu.VMEM((line,) + block, BF16),
            pltpu.VMEM((line,) + block, BF16),
            pltpu.VMEM((line,) + block, BF16),
            pltpu.VMEM((line,) + block, BF16),
            pltpu.VMEM((line,) + block, BF16),
            pltpu.VMEM(block, F32),
            dma((n,)), dma((4,)), dma((5,)),
            dma((2 * n,)), dma((2 * line,)), dma((2 * line,)), dma((2 * line,)), dma((4 * line,)),
            dma((n,)), dma((n,)), dma((n,)), dma((n,)), dma((n,)), dma((n,)),
            dma((2 * line,)), dma((2 * line,)), dma((2 * line,)), dma((2 * line,)), dma((2 * line,)),
            dma((2 * line,)), dma((2 * line,)),
        ],
        compiler_params=pltpu.CompilerParams(
            collective_id=0, has_side_effects=True, vmem_limit_bytes=62 * 2**20
        ),
        cost_estimate=pl.CostEstimate(
            flops=4 * rows * w_query.size, bytes_accessed=4 * w_query.size, transcendentals=0
        ),
    )(
        lengths, key_scales, value_scales, stream, norm_gain.reshape(1, -1),
        w_query, w_keyval.T, w_out, key_cache, value_cache,
    )


def per_device(n, *args):
    stream, _, w_query, w_keyval, _, lengths, key_cache, *_ = args
    rows, width = stream.shape
    local_rows = lengths.shape[0]
    qcols, kv_cols = w_query.shape[1], w_keyval.shape[1]
    tiles = (
        n % 4 == 0 and n >= 8 and n % KVH == 0 and width % 128 == 0 and qcols % HD == 0
        and HD % kv_cols == 0 and rows % 32 == 0 and rows <= 128
        and 8 % local_rows == 0
        and (qcols // HD + 1) * local_rows % 16 == 0
        and key_cache.shape[1] // 128 == args[8].shape[1]
    )
    return fused_device(n, *args) if tiles else plain_device(*args)


def solution(mesh):
    return jax.shard_map(
        functools.partial(per_device, mesh.shape["out"]),
        mesh=mesh,
        in_specs=(
            P("groups", "out"),
            P(),
            P(None, "out"),
            P(None, "out"),
            P("out", None),
            P(("groups", "out")),
            P(("groups", "out"), None, None),
            P(("groups", "out"), None, None),
            P(("groups", "out"), None, None),
            P(("groups", "out"), None, None),
        ),
        out_specs=P("groups", "out"),
        check_vma=False,
    )
```

```python
import functools
import math

import jax
import jax.numpy as jnp
from jax import lax
from jax.experimental import pallas as pl
from jax.experimental.pallas import tpu as pltpu
from jax.sharding import PartitionSpec as P

HQ = 48
KVH = 4
HD = 128


rope_base = 1000000.0
norm_eps = 1e-05


def rotate(vec, position):
    half = vec.shape[-1] // 2
    index = jnp.arange(half, dtype=jnp.float32)
    freq = jnp.exp(index * (-2.0 * math.log(rope_base) / vec.shape[-1]))
    angle = position * freq
    cosine = jnp.cos(angle)
    sine = jnp.sin(angle)
    first = vec[..., :half]
    second = vec[..., half:]
    return jnp.concatenate(
        [first * cosine - second * sine, second * cosine + first * sine], axis=-1
    )


def dequant(cache, scales):
    rows, span, width = cache.shape
    blocks = scales.shape[1]
    factor = jnp.exp2(scales.astype(jnp.float32)).astype(jnp.bfloat16)
    shaped = cache.reshape(rows, blocks, span // blocks, KVH, width // KVH)
    return (shaped * factor[:, :, None, :, None]).reshape(rows, span, KVH, width // KVH)


def plain_device(
    stream,
    norm_gain,
    w_query,
    w_keyval,
    w_out,
    lengths,
    key_cache,
    value_cache,
    key_scales,
    value_scales,
):
    local_rows = lengths.shape[0]
    xf = stream.astype(jnp.float32)
    whole = lax.all_gather(stream, "out", axis=1, tiled=True).astype(jnp.float32)
    meansq = jnp.mean(whole * whole, axis=-1, keepdims=True)
    normed = (whole * lax.rsqrt(meansq + norm_eps) * norm_gain).astype(jnp.bfloat16)
    q_local = jnp.dot(normed, w_query, preferred_element_type=jnp.float32).astype(jnp.bfloat16)
    kv_local = jnp.dot(normed, w_keyval, preferred_element_type=jnp.float32).astype(jnp.bfloat16)
    q_rows, kv_rows = (
        lax.all_to_all(q_local, "out", split_axis=0, concat_axis=1, tiled=True),
        lax.all_to_all(kv_local, "out", split_axis=0, concat_axis=1, tiled=True),
    )
    position = lengths.astype(jnp.float32)[:, None, None]
    rotated = rotate(q_rows.astype(jnp.float32).reshape(local_rows, HQ, HD), position).astype(
        jnp.bfloat16
    )
    rotated = rotated.reshape(local_rows, KVH, HQ // KVH, HD)
    new_key = rotate(
        kv_rows[:, : KVH * HD].astype(jnp.float32).reshape(local_rows, KVH, HD), position
    ).astype(jnp.bfloat16)
    new_value = kv_rows[:, KVH * HD :].reshape(local_rows, KVH, HD)
    factor = HD ** (-0.5)
    own = jnp.einsum("rkgd,rkd->rkg", rotated, new_key, preferred_element_type=jnp.float32) * factor
    span = key_cache.shape[1]
    scores = (
        jnp.einsum(
            "rkgd,rjkd->rkgj",
            rotated,
            dequant(key_cache, key_scales),
            preferred_element_type=jnp.float32,
        )
        * factor
    )
    valid = jnp.arange(span, dtype=jnp.int32)[None, :] < lengths[:, None]
    scores = jnp.where(valid[:, None, None, :], scores, -jnp.inf)
    top = jnp.maximum(jnp.max(scores, axis=-1), own)
    weights = jnp.exp(scores - top[..., None])
    own_weight = jnp.exp(own - top)
    total = jnp.sum(weights, axis=-1) + own_weight
    own_rounded = lax.optimization_barrier(own_weight.astype(jnp.bfloat16)).astype(jnp.float32)
    summed = jnp.einsum(
        "rkgj,rjkd->rkgd",
        weights.astype(jnp.bfloat16),
        dequant(value_cache, value_scales),
        preferred_element_type=jnp.float32,
    )
    summed = summed + own_rounded[..., None] * new_value.astype(jnp.float32)[:, :, None, :]
    attended = (summed / total[..., None]).astype(jnp.bfloat16).reshape(local_rows, HQ * HD)
    heads = lax.all_to_all(attended, "out", split_axis=1, concat_axis=0, tiled=True)
    partial_terms = jnp.dot(heads, w_out, preferred_element_type=jnp.float32)
    projected = lax.psum_scatter(partial_terms, "out", scatter_dimension=1, tiled=True)
    return (xf + projected).astype(jnp.bfloat16)


MESH = pl.DeviceIdType.MESH
F32 = jnp.float32
BF16 = jnp.bfloat16
CONTRACT_LAST = (((1,), (1,)), ((), ()))


def fused_kernel(
    n, rows, width, local_rows, span,
    len_ref, ks_ref, vs_ref,
    x_hbm, gain_hbm, wq_hbm, wkv_hbm, wo_hbm, kc_hbm, vc_hbm,
    out_ref,
    x_ref, gain_ref, cos_ref, sin_ref, kfac, vfac, wq, wkv, wo, kc, vc, xbuf, ssend, sbuf, accq, pk, qsend, qbuf, asend, abuf, heads,
    core_sb, core_rb, y_sb, y_rb, z_sb, up_rb, dn_rb, heads_sum,
    wq_sem, wo_sem, w_sem,
    ag_recv, ag_up, ag_dn, ag_y, ag_core,
    ss_send, ss_recv, q_send, q_recv, a_send, a_recv,
    core_send, core_recv, y_send, y_recv, z_send, up_recv, dn_recv,
):
    line = n // 4
    qcols = heads.shape[1]
    kv_cols = wkv_hbm.shape[0]
    own_heads = qcols // HD
    tile = qbuf.shape[1]
    per_head = n // KVH
    qrows = per_head * tile
    me = lax.axis_index("out")
    grp = lax.axis_index("groups")
    a = me // 4
    b = (me // 2) % 2
    c = me % 2

    def at(pos, bb, cc):
        return (pos * 2 + bb) * 2 + cc

    up, down = at(a + 1, b, c), at(a - 1, b, c)
    ypeer, cpeer = at(a, 1 - b, c), at(a, b, 1 - c)
    low, high = a, line - 1 - a
    least = jnp.minimum(low, high)

    def ranked(m):
        d = (m + 1) // 2
        near = jnp.where(m % 2 == 1, a - d, a + d)
        far = jnp.where(high > low, a + (m - least), a - (m - least))
        return jnp.where(m <= 2 * least, near, far)

    def remote(src, dst, ssem, rsem, to):
        return pltpu.make_async_remote_copy(
            src_ref=src, dst_ref=dst, send_sem=ssem, recv_sem=rsem,
            device_id=(grp, to), device_id_type=MESH,
        )

    def wq_copy(i):
        at_rows = pl.ds(pl.multiple_of(i * width, width), width)
        return pltpu.make_async_copy(wq_hbm.at[at_rows], wq.at[at_rows, pl.ds(0, qcols)], wq_sem.at[i])

    wo_parts = wo_sem.shape[0]
    wo_rows = wo.shape[0] // wo_parts

    def wo_copy(i):
        at_rows = pl.ds(i * wo_rows, wo_rows)
        return pltpu.make_async_copy(wo_hbm.at[at_rows], wo.at[at_rows], wo_sem.at[i])

    wkv_copy = pltpu.make_async_copy(wkv_hbm, wkv.at[pl.ds(0, kv_cols)], w_sem.at[0])
    kc_copy = pltpu.make_async_copy(kc_hbm, kc, w_sem.at[1])
    vc_copy = pltpu.make_async_copy(vc_hbm, vc, w_sem.at[2])

    x_copy = pltpu.make_async_copy(x_hbm, x_ref, w_sem.at[3])
    gain_copy = pltpu.make_async_copy(gain_hbm, gain_ref, w_sem.at[4])
    x_copy.start()
    gain_copy.start()

    barrier = pltpu.get_barrier_semaphore()

    def others(body):
        def step(i, carry):
            body(lax.rem(me + i, n))
            return carry
        lax.fori_loop(1, n, step, 0)

    others(lambda o: pl.semaphore_signal(barrier, inc=1, device_id=(grp, o), device_id_type=MESH))

    wkv_copy.start()
    if kv_cols < HD:
        wkv[kv_cols:, :] = jnp.zeros((HD - kv_cols, n * width), BF16)

    def start_wq(m, carry):
        pos = ranked(m)
        for bb, cc in ((b, c), (b, 1 - c), (1 - b, c), (1 - b, 1 - c)):
            wq_copy(at(pos, bb, cc)).start()
        return carry
    lax.fori_loop(0, line, start_wq, 0)

    x_copy.wait()
    xbuf[me] = x_ref[...]
    xf = x_ref[...].astype(F32)
    square = jnp.sum(xf * xf, axis=1, keepdims=True)
    spread = jnp.transpose(jnp.broadcast_to(square, (rows, 128)))
    ssend[...] = jnp.zeros_like(ssend)
    ssend[:, 0:rows] = spread[0:8, :]
    sbuf[me] = ssend[...]
    accq[...] = jnp.zeros_like(accq)

    pl.semaphore_wait(barrier, n - 1)

    half_rows = rows // 2

    def ag_copy(block, h, ssem, to):
        part = xbuf.at[block, pl.ds(h * half_rows, half_rows)]
        return remote(part, part, ssem, ag_recv.at[2 * block + h], to)

    def ag_wait(block, h):
        ag_copy(block, h, ag_core.at[0], cpeer).wait_recv()

    def spread_line(pos, h):
        block = at(pos, b, c)

        @pl.when((pos <= a) & (a < line - 1))
        def _():
            ag_copy(block, h, ag_up.at[2 * pos + h], up).start()

        @pl.when((pos >= a) & (a > 0))
        def _():
            ag_copy(block, h, ag_dn.at[2 * pos + h], down).start()

        ag_copy(block, h, ag_y.at[2 * pos + h], ypeer).start()
        ag_copy(block, h, ag_core.at[2 * pos + h], cpeer).start()

    def ss_copy(o, slot):
        return remote(ssend, sbuf.at[slot], ss_send.at[o], ss_recv.at[slot], o)

    others(lambda o: ss_copy(o, me).start())
    for h in range(2):
        spread_line(a, h)
    ridx = lax.broadcasted_iota(jnp.int32, (qrows, 128), 0) % local_rows
    pick = lax.broadcasted_iota(jnp.int32, (qrows, tile), 0) % local_rows
    pick = pick + own_heads * local_rows == lax.broadcasted_iota(jnp.int32, (qrows, tile), 1)
    pick = pick.astype(F32).astype(BF16)
    blocks = span // 128
    few = lax.broadcasted_iota(jnp.int32, (8, 128), 0) % local_rows
    lane8 = lax.broadcasted_iota(jnp.int32, (8, 128), 1)

    def by_row(values):
        res = jnp.full((8, 128), values[0])
        for r in range(1, local_rows):
            res = jnp.where(few == r, values[r], res)
        return res

    def tall(v):
        return jnp.concatenate([v] * (qrows // 8), axis=0)

    limit8 = by_row([len_ref[r] for r in range(local_rows)])
    freq = jnp.exp((lane8 % (HD // 2)).astype(F32) * (-2.0 * math.log(rope_base) / HD))
    angle = limit8.astype(F32) * freq
    cos_ref[...] = jnp.cos(angle)
    sin_ref[...] = jnp.where(lane8 < HD // 2, -1.0, 1.0) * jnp.sin(angle)
    for k in range(KVH):
        for u in range(blocks):
            for ref, table in ((ks_ref, kfac), (vs_ref, vfac)):
                power = by_row([ref[r, u, k] for r in range(local_rows)]).astype(F32)
                table[k * blocks + u] = jnp.exp2(power).astype(BF16).astype(F32)

    wkv_copy.wait()

    def turn(i, carry):
        start = pl.multiple_of(i * width, width)
        turned = jnp.transpose(wkv[:, pl.ds(start, width)].astype(F32)).astype(BF16)
        wq[pl.ds(start, width), qcols:] = turned
        return carry
    lax.fori_loop(0, n, turn, 0)
    others(lambda o: ss_copy(o, o).wait_recv())
    total_sq = jnp.sum(sbuf[...], axis=0)[0:1, :]
    column = jnp.transpose(jnp.broadcast_to(total_sq, (128, 128)))[0:rows, 0:1]
    scale = lax.rsqrt(column * (1.0 / (n * width)) + norm_eps)
    gain_copy.wait()

    def project(block):
        wq_copy(block).wait()
        start = pl.multiple_of(block * width, width)
        normed = (xbuf[block].astype(F32) * scale * gain_ref[:, pl.ds(start, width)]).astype(BF16)
        accq[...] += jnp.dot(normed, wq[pl.ds(start, width), :], preferred_element_type=F32)

    def take_line(m, h):
        @pl.when(m < line)
        def _():
            pos = ranked(m)
            ag_wait(at(pos, b, c), h)
            spread_line(pos, h)

    def take_pair(m, h):
        pos = ranked(m)
        block = at(pos, 1 - b, c)
        ag_wait(block, h)
        ag_copy(block, h, ag_core.at[2 * (line + pos) + h], cpeer).start()

    project(me)

    def gather_step(m, carry):
        take_line(m, 0)
        take_pair(m - 1, 0)
        cblock = at(ranked(m - 1), b, 1 - c)
        for h in range(2):
            ag_wait(cblock, h)
        project(cblock)
        take_line(m, 1)
        take_pair(m - 1, 1)
        project(at(ranked(m - 1), 1 - b, c))

        @pl.when(m < line)
        def _():
            project(at(ranked(m), b, c))

        @pl.when(m > 1)
        def _():
            block = at(ranked(m - 2), 1 - b, 1 - c)
            for h in range(2):
                ag_wait(block, h)
            project(block)

        @pl.when(m == 1)
        def _():
            kc_copy.start()
            vc_copy.start()
            for i in range(wo_parts):
                wo_copy(i).start()
        return carry
    lax.fori_loop(1, line + 1, gather_step, 0)
    last = at(ranked(line - 1), 1 - b, 1 - c)
    for h in range(2):
        ag_wait(last, h)
    project(last)

    pk[...] = jnp.zeros_like(pk)
    q_all = accq[...]
    kv_all = q_all[:, qcols:qcols + kv_cols]
    for j in range(n):
        mine = slice(j * local_rows, (j + 1) * local_rows)
        for g in range(own_heads):
            pk[j, g * local_rows:(g + 1) * local_rows, :] = q_all[mine, g * HD:(g + 1) * HD]
        pk[j, own_heads * local_rows:tile, 0:kv_cols] = kv_all[mine, :]
    qsend[...] = pk[...].astype(BF16)

    def q_copy(o, slot):
        return remote(qsend.at[o], qbuf.at[slot], q_send.at[o], q_recv.at[slot], o)

    others(lambda o: q_copy(o, me).start())
    qbuf[me] = qsend[me]

    limit = tall(limit8)
    lane = lax.broadcasted_iota(jnp.int32, (qrows, 128), 1)
    cosine, sine = tall(cos_ref[...]), tall(sin_ref[...])

    def rotated(v):
        return (v * cosine + pltpu.roll(v, HD // 2, 1) * sine).astype(BF16)

    kc_copy.wait()
    vc_copy.wait()
    others(lambda o: q_copy(o, o).wait_recv())

    pieces = HD // kv_cols
    factor = HD ** (-0.5)

    def new_head(first):
        res = None
        for p in range(pieces):
            part = jnp.dot(pick, qbuf[first + p], preferred_element_type=F32)
            part = part if p == 0 else pltpu.roll(part, p * kv_cols, 1)
            res = part if res is None else res + part
        return res

    for k in range(KVH):
        at_k = slice(k * HD, (k + 1) * HD)
        query = rotated(qbuf[k * per_head:(k + 1) * per_head].astype(F32).reshape(qrows, HD))
        new_key = rotated(new_head(k * pieces)).astype(F32)
        new_value = new_head((KVH + k) * pieces)
        own = jnp.sum(query.astype(F32) * new_key, axis=1, keepdims=True) * factor
        score = None
        for r in range(local_rows):
            one = lax.dot_general(query, kc[r, :, at_k], CONTRACT_LAST, preferred_element_type=F32)
            cut = [one[:, 128 * u:128 * (u + 1)] for u in range(blocks)]
            score = cut if r == 0 else [jnp.where(ridx == r, x, y) for x, y in zip(cut, score)]
        highest = None
        for u in range(blocks):
            scales = tall(kfac[k * blocks + u])
            score[u] = jnp.where(lane + 128 * u < limit, score[u] * scales * factor, -jnp.inf)
            highest = score[u] if u == 0 else jnp.maximum(highest, score[u])
        top = jnp.maximum(own, jnp.max(highest, axis=1, keepdims=True))
        own_weight = jnp.exp(own - top)
        added = None
        weights = []
        for u in range(blocks):
            weight = jnp.exp(score[u] - top)
            added = weight if u == 0 else added + weight
            scales = tall(vfac[k * blocks + u])
            weights.append((weight.astype(BF16).astype(F32) * scales).astype(BF16))
        total = own_weight + jnp.sum(added, axis=1, keepdims=True)
        weights = jnp.concatenate(weights, axis=1)
        summed = None
        for r in range(local_rows):
            one = jnp.dot(weights, vc[r, :, at_k], preferred_element_type=F32)
            summed = one if r == 0 else jnp.where(ridx == r, one, summed)
        summed = summed + own_weight.astype(BF16).astype(F32) * new_value
        result = (summed / total).astype(BF16)
        for s in range(per_head):
            asend[k * per_head + s] = result[s * tile:(s + 1) * tile, :]

    def a_copy(o, slot):
        return remote(asend.at[o], abuf.at[slot], a_send.at[o], a_recv.at[slot], o)

    others(lambda o: a_copy(o, me).start())
    abuf[me] = asend[me]
    for i in range(wo_parts):
        wo_copy(i).wait()
    others(lambda o: a_copy(o, o).wait_recv())
    pk[...] = abuf[...].astype(F32)
    for j in range(n):
        for g in range(own_heads):
            heads[j * local_rows:(j + 1) * local_rows, g * HD:(g + 1) * HD] = (
                pk[j, g * local_rows:(g + 1) * local_rows, :]
            )
    attended = heads[...].astype(BF16)

    def partial(block):
        start = pl.multiple_of(block * width, width)
        return jnp.dot(attended, wo[:, pl.ds(start, width)], preferred_element_type=F32)

    def core_copy(slot):
        return remote(core_sb.at[slot], core_rb.at[slot], core_send.at[slot], core_recv.at[slot], cpeer)

    def half_of(ref, pos, h):
        return ref.at[pos, pl.ds(h * half_rows, half_rows)]

    def y_copy(pos, h):
        i = 2 * pos + h
        return remote(half_of(y_sb, pos, h), half_of(y_rb, pos, h), y_send.at[i], y_recv.at[i], ypeer)

    def up_copy(pos, h):
        i = 2 * pos + h
        return remote(half_of(z_sb, pos, h), half_of(up_rb, pos, h), z_send.at[i], up_recv.at[i], up)

    def dn_copy(pos, h):
        i = 2 * pos + h
        return remote(half_of(z_sb, pos, h), half_of(dn_rb, pos, h), z_send.at[i], dn_recv.at[i], down)

    def to_core_far(pos):
        core_sb[line + pos] = partial(at(pos, 1 - b, 1 - c)).astype(BF16)
        core_copy(line + pos).start()

    def to_pair(pos):
        term = partial(at(pos, 1 - b, c))
        core_copy(line + pos).wait_recv()
        y_sb[pos] = (term + core_rb[line + pos].astype(F32)).astype(BF16)
        for h in range(2):
            y_copy(pos, h).start()

    def to_core_near(pos):
        core_sb[pos] = partial(at(pos, b, 1 - c)).astype(BF16)
        core_copy(pos).start()

    def to_line(pos):
        term = partial(at(pos, b, c))
        core_copy(pos).wait_recv()
        heads_sum[...] = term + core_rb[pos].astype(F32)
        for h in range(2):
            part = pl.ds(h * half_rows, half_rows)
            y_copy(pos, h).wait_recv()
            heads_sum[part] += y_rb[pos, part].astype(F32)

            @pl.when((pos >= a) & (a > 0))
            def _():
                up_copy(pos, h).wait_recv()
                heads_sum[part] += up_rb[pos, part].astype(F32)

            @pl.when((pos <= a) & (a < line - 1))
            def _():
                dn_copy(pos, h).wait_recv()
                heads_sum[part] += dn_rb[pos, part].astype(F32)

            @pl.when(pos > a)
            def _():
                z_sb[pos, part] = heads_sum[part].astype(BF16)
                up_copy(pos, h).start()

            @pl.when(pos < a)
            def _():
                z_sb[pos, part] = heads_sum[part].astype(BF16)
                dn_copy(pos, h).start()

            @pl.when(pos == a)
            def _():
                out_ref[part] = (x_ref[part].astype(F32) + heads_sum[part]).astype(BF16)

    def far(m):
        return ranked(line - 1 - m)

    to_core_far(far(0))

    def pair_step(m, carry):
        @pl.when(m + 1 < line)
        def _():
            to_core_far(far(m + 1))

        to_pair(far(m))
        return carry
    lax.fori_loop(0, line, pair_step, 0)

    to_core_near(far(0))

    def sum_step(m, carry):
        @pl.when(m + 1 < line)
        def _():
            to_core_near(far(m + 1))

        to_line(far(m))
        return carry
    lax.fori_loop(0, line, sum_step, 0)

    def sent_gather(i, carry):
        pos, h = i // 2, i % 2
        block = at(pos, b, c)

        @pl.when((pos <= a) & (a < line - 1))
        def _():
            ag_copy(block, h, ag_up.at[2 * pos + h], up).wait_send()

        @pl.when((pos >= a) & (a > 0))
        def _():
            ag_copy(block, h, ag_dn.at[2 * pos + h], down).wait_send()

        ag_copy(block, h, ag_y.at[2 * pos + h], ypeer).wait_send()
        ag_copy(block, h, ag_core.at[2 * pos + h], cpeer).wait_send()
        ag_copy(at(pos, 1 - b, c), h, ag_core.at[2 * (line + pos) + h], cpeer).wait_send()
        y_copy(pos, h).wait_send()

        @pl.when(pos > a)
        def _():
            up_copy(pos, h).wait_send()

        @pl.when(pos < a)
        def _():
            dn_copy(pos, h).wait_send()
        return carry
    lax.fori_loop(0, 2 * line, sent_gather, 0)

    def sent(pos, carry):
        core_copy(pos).wait_send()
        core_copy(line + pos).wait_send()
        return carry
    lax.fori_loop(0, line, sent, 0)

    def sent_others(o):
        ss_copy(o, o).wait_send()
        q_copy(o, o).wait_send()
        a_copy(o, o).wait_send()
    others(sent_others)


def fused_device(
    n, stream, norm_gain, w_query, w_keyval, w_out, lengths, key_cache, value_cache,
    key_scales, value_scales,
):
    rows, width = stream.shape
    local_rows = lengths.shape[0]
    span = key_cache.shape[1]
    line = n // 4
    qcols = w_query.shape[1]
    tile = (qcols // HD + 1) * local_rows
    vmem = pl.BlockSpec(memory_space=pltpu.VMEM)
    smem = pl.BlockSpec(memory_space=pltpu.SMEM)
    hbm = pl.BlockSpec(memory_space=pl.ANY)
    block = (rows, width)
    dma = pltpu.SemaphoreType.DMA
    return pl.pallas_call(
        functools.partial(fused_kernel, n, rows, width, local_rows, span),
        out_shape=jax.ShapeDtypeStruct(block, BF16),
        in_specs=[smem] * 3 + [hbm] * 7,
        out_specs=vmem,
        scratch_shapes=[
            pltpu.VMEM(block, BF16),
            pltpu.VMEM((1, n * width), F32),
            pltpu.VMEM((8, HD), F32),
            pltpu.VMEM((8, HD), F32),
            pltpu.VMEM((KVH * (span // 128), 8, 128), F32),
            pltpu.VMEM((KVH * (span // 128), 8, 128), F32),
            pltpu.VMEM((n * width, qcols + HD), BF16),
            pltpu.VMEM((HD, n * width), BF16),
            pltpu.VMEM(w_out.shape, BF16),
            pltpu.VMEM(key_cache.shape, BF16),
            pltpu.VMEM(value_cache.shape, BF16),
            pltpu.VMEM((n,) + block, BF16),
            pltpu.VMEM((8, 128), F32),
            pltpu.VMEM((n, 8, 128), F32),
            pltpu.VMEM((rows, qcols + HD), F32),
            pltpu.VMEM((n, tile, HD), F32),
            pltpu.VMEM((n, tile, HD), BF16),
            pltpu.VMEM((n, tile, HD), BF16),
            pltpu.VMEM((n, tile, HD), BF16),
            pltpu.VMEM((n, tile, HD), BF16),
            pltpu.VMEM((rows, qcols), F32),
            pltpu.VMEM((2 * line,) + block, BF16),
            pltpu.VMEM((2 * line,) + block, BF16),
            pltpu.VMEM((line,) + block, BF16),
            pltpu.VMEM((line,) + block, BF16),
            pltpu.VMEM((line,) + block, BF16),
            pltpu.VMEM((line,) + block, BF16),
            pltpu.VMEM((line,) + block, BF16),
            pltpu.VMEM(block, F32),
            dma((n,)), dma((4,)), dma((5,)),
            dma((2 * n,)), dma((2 * line,)), dma((2 * line,)), dma((2 * line,)), dma((4 * line,)),
            dma((n,)), dma((n,)), dma((n,)), dma((n,)), dma((n,)), dma((n,)),
            dma((2 * line,)), dma((2 * line,)), dma((2 * line,)), dma((2 * line,)), dma((2 * line,)),
            dma((2 * line,)), dma((2 * line,)),
        ],
        compiler_params=pltpu.CompilerParams(
            collective_id=0, has_side_effects=True, vmem_limit_bytes=62 * 2**20
        ),
        cost_estimate=pl.CostEstimate(
            flops=4 * rows * w_query.size, bytes_accessed=4 * w_query.size, transcendentals=0
        ),
    )(
        lengths, key_scales, value_scales, stream, norm_gain.reshape(1, -1),
        w_query, w_keyval.T, w_out, key_cache, value_cache,
    )


def per_device(n, *args):
    stream, _, w_query, w_keyval, _, lengths, key_cache, *_ = args
    rows, width = stream.shape
    local_rows = lengths.shape[0]
    qcols, kv_cols = w_query.shape[1], w_keyval.shape[1]
    tiles = (
        n % 4 == 0 and n >= 8 and n % KVH == 0 and width % 128 == 0 and qcols % HD == 0
        and HD % kv_cols == 0 and rows % 32 == 0 and rows <= 128
        and 8 % local_rows == 0
        and (qcols // HD + 1) * local_rows % 16 == 0
        and key_cache.shape[1] // 128 == args[8].shape[1]
    )
    return fused_device(n, *args) if tiles else plain_device(*args)


def solution(mesh):
    return jax.shard_map(
        functools.partial(per_device, mesh.shape["out"]),
        mesh=mesh,
        in_specs=(
            P("groups", "out"),
            P(),
            P(None, "out"),
            P(None, "out"),
            P("out", None),
            P(("groups", "out")),
            P(("groups", "out"), None, None),
            P(("groups", "out"), None, None),
            P(("groups", "out"), None, None),
            P(("groups", "out"), None, None),
        ),
        out_specs=P("groups", "out"),
        check_vma=False,
    )
```

```python
import functools
import math

import jax
import jax.numpy as jnp
from jax import lax
from jax.experimental import pallas as pl
from jax.experimental.pallas import tpu as pltpu
from jax.sharding import PartitionSpec as P

HQ = 48
KVH = 4
HD = 128


rope_base = 1000000.0
norm_eps = 1e-05


def rotate(vec, position):
    half = vec.shape[-1] // 2
    index = jnp.arange(half, dtype=jnp.float32)
    freq = jnp.exp(index * (-2.0 * math.log(rope_base) / vec.shape[-1]))
    angle = position * freq
    cosine = jnp.cos(angle)
    sine = jnp.sin(angle)
    first = vec[..., :half]
    second = vec[..., half:]
    return jnp.concatenate(
        [first * cosine - second * sine, second * cosine + first * sine], axis=-1
    )


def dequant(cache, scales):
    rows, span, width = cache.shape
    blocks = scales.shape[1]
    factor = jnp.exp2(scales.astype(jnp.float32)).astype(jnp.bfloat16)
    shaped = cache.reshape(rows, blocks, span // blocks, KVH, width // KVH)
    return (shaped * factor[:, :, None, :, None]).reshape(rows, span, KVH, width // KVH)


def plain_device(
    stream,
    norm_gain,
    w_query,
    w_keyval,
    w_out,
    lengths,
    key_cache,
    value_cache,
    key_scales,
    value_scales,
):
    local_rows = lengths.shape[0]
    xf = stream.astype(jnp.float32)
    whole = lax.all_gather(stream, "out", axis=1, tiled=True).astype(jnp.float32)
    meansq = jnp.mean(whole * whole, axis=-1, keepdims=True)
    normed = (whole * lax.rsqrt(meansq + norm_eps) * norm_gain).astype(jnp.bfloat16)
    q_local = jnp.dot(normed, w_query, preferred_element_type=jnp.float32).astype(jnp.bfloat16)
    kv_local = jnp.dot(normed, w_keyval, preferred_element_type=jnp.float32).astype(jnp.bfloat16)
    q_rows, kv_rows = (
        lax.all_to_all(q_local, "out", split_axis=0, concat_axis=1, tiled=True),
        lax.all_to_all(kv_local, "out", split_axis=0, concat_axis=1, tiled=True),
    )
    position = lengths.astype(jnp.float32)[:, None, None]
    rotated = rotate(q_rows.astype(jnp.float32).reshape(local_rows, HQ, HD), position).astype(
        jnp.bfloat16
    )
    rotated = rotated.reshape(local_rows, KVH, HQ // KVH, HD)
    new_key = rotate(
        kv_rows[:, : KVH * HD].astype(jnp.float32).reshape(local_rows, KVH, HD), position
    ).astype(jnp.bfloat16)
    new_value = kv_rows[:, KVH * HD :].reshape(local_rows, KVH, HD)
    factor = HD ** (-0.5)
    own = jnp.einsum("rkgd,rkd->rkg", rotated, new_key, preferred_element_type=jnp.float32) * factor
    span = key_cache.shape[1]
    scores = (
        jnp.einsum(
            "rkgd,rjkd->rkgj",
            rotated,
            dequant(key_cache, key_scales),
            preferred_element_type=jnp.float32,
        )
        * factor
    )
    valid = jnp.arange(span, dtype=jnp.int32)[None, :] < lengths[:, None]
    scores = jnp.where(valid[:, None, None, :], scores, -jnp.inf)
    top = jnp.maximum(jnp.max(scores, axis=-1), own)
    weights = jnp.exp(scores - top[..., None])
    own_weight = jnp.exp(own - top)
    total = jnp.sum(weights, axis=-1) + own_weight
    own_rounded = lax.optimization_barrier(own_weight.astype(jnp.bfloat16)).astype(jnp.float32)
    summed = jnp.einsum(
        "rkgj,rjkd->rkgd",
        weights.astype(jnp.bfloat16),
        dequant(value_cache, value_scales),
        preferred_element_type=jnp.float32,
    )
    summed = summed + own_rounded[..., None] * new_value.astype(jnp.float32)[:, :, None, :]
    attended = (summed / total[..., None]).astype(jnp.bfloat16).reshape(local_rows, HQ * HD)
    heads = lax.all_to_all(attended, "out", split_axis=1, concat_axis=0, tiled=True)
    partial_terms = jnp.dot(heads, w_out, preferred_element_type=jnp.float32)
    projected = lax.psum_scatter(partial_terms, "out", scatter_dimension=1, tiled=True)
    return (xf + projected).astype(jnp.bfloat16)


MESH = pl.DeviceIdType.MESH
F32 = jnp.float32
BF16 = jnp.bfloat16
CONTRACT_LAST = (((1,), (1,)), ((), ()))


def fused_kernel(
    n, rows, width, local_rows, span,
    len_ref, ks_ref, vs_ref,
    x_hbm, gain_hbm, wq_hbm, wkv_hbm, wo_hbm, kc_hbm, vc_hbm,
    out_ref,
    x_ref, gain_ref, cos_ref, sin_ref, kfac, vfac, wq, wkv, wo, kc, vc, xbuf, ssend, sbuf, accq, pk, qsend, qbuf, asend, abuf, heads,
    core_sb, core_rb, y_sb, y_rb, z_sb, up_rb, dn_rb, heads_sum,
    wq_sem, wo_sem, w_sem,
    ag_recv, ag_up, ag_dn, ag_y, ag_core,
    ss_send, ss_recv, q_send, q_recv, a_send, a_recv,
    core_send, core_recv, y_send, y_recv, z_send, up_recv, dn_recv,
):
    line = n // 4
    qcols = heads.shape[1]
    kv_cols = wkv_hbm.shape[0]
    own_heads = qcols // HD
    tile = qbuf.shape[1]
    per_head = n // KVH
    qrows = per_head * tile
    me = lax.axis_index("out")
    grp = lax.axis_index("groups")
    a = me // 4
    b = (me // 2) % 2
    c = me % 2

    def at(pos, bb, cc):
        return (pos * 2 + bb) * 2 + cc

    up, down = at(a + 1, b, c), at(a - 1, b, c)
    ypeer, cpeer = at(a, 1 - b, c), at(a, b, 1 - c)
    low, high = a, line - 1 - a
    least = jnp.minimum(low, high)

    def ranked(m):
        d = (m + 1) // 2
        near = jnp.where(m % 2 == 1, a - d, a + d)
        far = jnp.where(high > low, a + (m - least), a - (m - least))
        return jnp.where(m <= 2 * least, near, far)

    def remote(src, dst, ssem, rsem, to):
        return pltpu.make_async_remote_copy(
            src_ref=src, dst_ref=dst, send_sem=ssem, recv_sem=rsem,
            device_id=(grp, to), device_id_type=MESH,
        )

    def wq_copy(i):
        at_rows = pl.ds(pl.multiple_of(i * width, width), width)
        return pltpu.make_async_copy(wq_hbm.at[at_rows], wq.at[at_rows, pl.ds(0, qcols)], wq_sem.at[i])

    wo_parts = wo_sem.shape[0]
    wo_rows = wo.shape[0] // wo_parts

    def wo_copy(i):
        at_rows = pl.ds(i * wo_rows, wo_rows)
        return pltpu.make_async_copy(wo_hbm.at[at_rows], wo.at[at_rows], wo_sem.at[i])

    wkv_copy = pltpu.make_async_copy(wkv_hbm, wkv.at[pl.ds(0, kv_cols)], w_sem.at[0])
    kc_copy = pltpu.make_async_copy(kc_hbm, kc, w_sem.at[1])
    vc_copy = pltpu.make_async_copy(vc_hbm, vc, w_sem.at[2])

    x_copy = pltpu.make_async_copy(x_hbm, x_ref, w_sem.at[3])
    gain_copy = pltpu.make_async_copy(gain_hbm, gain_ref, w_sem.at[4])
    x_copy.start()
    gain_copy.start()

    barrier = pltpu.get_barrier_semaphore()

    def others(body):
        def step(i, carry):
            body(lax.rem(me + i, n))
            return carry
        lax.fori_loop(1, n, step, 0)

    others(lambda o: pl.semaphore_signal(barrier, inc=1, device_id=(grp, o), device_id_type=MESH))

    wkv_copy.start()
    if kv_cols < HD:
        wkv[kv_cols:, :] = jnp.zeros((HD - kv_cols, n * width), BF16)

    def start_wq(m, carry):
        pos = ranked(m)
        for bb, cc in ((b, c), (b, 1 - c), (1 - b, c), (1 - b, 1 - c)):
            wq_copy(at(pos, bb, cc)).start()
        return carry
    lax.fori_loop(0, line, start_wq, 0)

    x_copy.wait()
    xbuf[me] = x_ref[...]
    xf = x_ref[...].astype(F32)
    square = jnp.sum(xf * xf, axis=1, keepdims=True)
    spread = jnp.transpose(jnp.broadcast_to(square, (rows, 128)))
    ssend[...] = jnp.zeros_like(ssend)
    ssend[:, 0:rows] = spread[0:8, :]
    sbuf[me] = ssend[...]
    accq[...] = jnp.zeros_like(accq)

    pl.semaphore_wait(barrier, n - 1)

    half_rows = rows // 2

    def ag_copy(block, h, ssem, to):
        part = xbuf.at[block, pl.ds(h * half_rows, half_rows)]
        return remote(part, part, ssem, ag_recv.at[2 * block + h], to)

    def ag_wait(block, h):
        ag_copy(block, h, ag_core.at[0], cpeer).wait_recv()

    def spread_line(pos, h):
        block = at(pos, b, c)

        @pl.when((pos <= a) & (a < line - 1))
        def _():
            ag_copy(block, h, ag_up.at[2 * pos + h], up).start()

        @pl.when((pos >= a) & (a > 0))
        def _():
            ag_copy(block, h, ag_dn.at[2 * pos + h], down).start()

        ag_copy(block, h, ag_y.at[2 * pos + h], ypeer).start()
        ag_copy(block, h, ag_core.at[2 * pos + h], cpeer).start()

    def ss_copy(o, slot):
        return remote(ssend, sbuf.at[slot], ss_send.at[o], ss_recv.at[slot], o)

    others(lambda o: ss_copy(o, me).start())
    for h in range(2):
        spread_line(a, h)
    ridx = lax.broadcasted_iota(jnp.int32, (qrows, 128), 0) % local_rows
    pick = lax.broadcasted_iota(jnp.int32, (qrows, tile), 0) % local_rows
    pick = pick + own_heads * local_rows == lax.broadcasted_iota(jnp.int32, (qrows, tile), 1)
    pick = pick.astype(F32).astype(BF16)
    blocks = span // 128
    few = lax.broadcasted_iota(jnp.int32, (8, 128), 0) % local_rows
    lane8 = lax.broadcasted_iota(jnp.int32, (8, 128), 1)

    def by_row(values):
        res = jnp.full((8, 128), values[0])
        for r in range(1, local_rows):
            res = jnp.where(few == r, values[r], res)
        return res

    def tall(v):
        return jnp.concatenate([v] * (qrows // 8), axis=0)

    limit8 = by_row([len_ref[r] for r in range(local_rows)])
    freq = jnp.exp((lane8 % (HD // 2)).astype(F32) * (-2.0 * math.log(rope_base) / HD))
    angle = limit8.astype(F32) * freq
    cos_ref[...] = jnp.cos(angle)
    sin_ref[...] = jnp.where(lane8 < HD // 2, -1.0, 1.0) * jnp.sin(angle)
    for k in range(KVH):
        for u in range(blocks):
            for ref, table in ((ks_ref, kfac), (vs_ref, vfac)):
                power = by_row([ref[r, u, k] for r in range(local_rows)]).astype(F32)
                table[k * blocks + u] = jnp.exp2(power).astype(BF16).astype(F32)

    def take_line(m, h):
        @pl.when(m < line)
        def _():
            pos = ranked(m)
            ag_wait(at(pos, b, c), h)
            spread_line(pos, h)

    def take_pair(m, h):
        @pl.when(m < line)
        def _():
            pos = ranked(m)
            block = at(pos, 1 - b, c)
            ag_wait(block, h)
            ag_copy(block, h, ag_core.at[2 * (line + pos) + h], cpeer).start()

    for h in range(2):
        take_line(1, h)
        take_pair(0, h)

    wkv_copy.wait()

    def turn(i, carry):
        start = pl.multiple_of(i * width, width)
        turned = jnp.transpose(wkv[:, pl.ds(start, width)].astype(F32)).astype(BF16)
        wq[pl.ds(start, width), qcols:] = turned
        return carry
    lax.fori_loop(0, n, turn, 0)
    others(lambda o: ss_copy(o, o).wait_recv())
    total_sq = jnp.sum(sbuf[...], axis=0)[0:1, :]
    column = jnp.transpose(jnp.broadcast_to(total_sq, (128, 128)))[0:rows, 0:1]
    scale = lax.rsqrt(column * (1.0 / (n * width)) + norm_eps)
    gain_copy.wait()

    def project(block):
        wq_copy(block).wait()
        start = pl.multiple_of(block * width, width)
        normed = (xbuf[block].astype(F32) * scale * gain_ref[:, pl.ds(start, width)]).astype(BF16)
        accq[...] += jnp.dot(normed, wq[pl.ds(start, width), :], preferred_element_type=F32)

    def gather_step(m, carry):
        prev = ranked(m - 1)
        project(at(prev, b, c))
        take_line(m + 1, 0)
        take_pair(m, 0)
        cblock = at(prev, b, 1 - c)
        for h in range(2):
            ag_wait(cblock, h)
        project(cblock)
        take_line(m + 1, 1)
        take_pair(m, 1)
        project(at(prev, 1 - b, c))

        @pl.when(m > 1)
        def _():
            block = at(ranked(m - 2), 1 - b, 1 - c)
            for h in range(2):
                ag_wait(block, h)
            project(block)

        @pl.when(m == 1)
        def _():
            kc_copy.start()
            vc_copy.start()
            for i in range(wo_parts):
                wo_copy(i).start()
        return carry
    lax.fori_loop(1, line + 1, gather_step, 0)
    last = at(ranked(line - 1), 1 - b, 1 - c)
    for h in range(2):
        ag_wait(last, h)
    project(last)

    pk[...] = jnp.zeros_like(pk)
    q_all = accq[...]
    kv_all = q_all[:, qcols:qcols + kv_cols]
    for j in range(n):
        mine = slice(j * local_rows, (j + 1) * local_rows)
        for g in range(own_heads):
            pk[j, g * local_rows:(g + 1) * local_rows, :] = q_all[mine, g * HD:(g + 1) * HD]
        pk[j, own_heads * local_rows:tile, 0:kv_cols] = kv_all[mine, :]
    qsend[...] = pk[...].astype(BF16)

    def q_copy(o, slot):
        return remote(qsend.at[o], qbuf.at[slot], q_send.at[o], q_recv.at[slot], o)

    others(lambda o: q_copy(o, me).start())
    qbuf[me] = qsend[me]
    def sent_gather(i, carry):
        pos, h = i // 2, i % 2
        block = at(pos, b, c)

        @pl.when((pos <= a) & (a < line - 1))
        def _():
            ag_copy(block, h, ag_up.at[2 * pos + h], up).wait_send()

        @pl.when((pos >= a) & (a > 0))
        def _():
            ag_copy(block, h, ag_dn.at[2 * pos + h], down).wait_send()

        ag_copy(block, h, ag_y.at[2 * pos + h], ypeer).wait_send()
        ag_copy(block, h, ag_core.at[2 * pos + h], cpeer).wait_send()
        ag_copy(at(pos, 1 - b, c), h, ag_core.at[2 * (line + pos) + h], cpeer).wait_send()
        return carry
    lax.fori_loop(0, 2 * line, sent_gather, 0)
    others(lambda o: ss_copy(o, o).wait_send())


    limit = tall(limit8)
    lane = lax.broadcasted_iota(jnp.int32, (qrows, 128), 1)
    cosine, sine = tall(cos_ref[...]), tall(sin_ref[...])

    def rotated(v):
        return (v * cosine + pltpu.roll(v, HD // 2, 1) * sine).astype(BF16)

    kc_copy.wait()
    vc_copy.wait()
    others(lambda o: q_copy(o, o).wait_recv())

    pieces = HD // kv_cols
    factor = HD ** (-0.5)

    def new_head(first):
        res = None
        for p in range(pieces):
            part = jnp.dot(pick, qbuf[first + p], preferred_element_type=F32)
            part = part if p == 0 else pltpu.roll(part, p * kv_cols, 1)
            res = part if res is None else res + part
        return res

    for k in range(KVH):
        at_k = slice(k * HD, (k + 1) * HD)
        query = rotated(qbuf[k * per_head:(k + 1) * per_head].astype(F32).reshape(qrows, HD))
        new_key = rotated(new_head(k * pieces)).astype(F32)
        new_value = new_head((KVH + k) * pieces)
        own = jnp.sum(query.astype(F32) * new_key, axis=1, keepdims=True) * factor
        score = None
        for r in range(local_rows):
            one = lax.dot_general(query, kc[r, :, at_k], CONTRACT_LAST, preferred_element_type=F32)
            cut = [one[:, 128 * u:128 * (u + 1)] for u in range(blocks)]
            score = cut if r == 0 else [jnp.where(ridx == r, x, y) for x, y in zip(cut, score)]
        highest = None
        for u in range(blocks):
            scales = tall(kfac[k * blocks + u])
            score[u] = jnp.where(lane + 128 * u < limit, score[u] * scales * factor, -jnp.inf)
            highest = score[u] if u == 0 else jnp.maximum(highest, score[u])
        top = jnp.maximum(own, jnp.max(highest, axis=1, keepdims=True))
        own_weight = jnp.exp(own - top)
        added = None
        weights = []
        for u in range(blocks):
            weight = jnp.exp(score[u] - top)
            added = weight if u == 0 else added + weight
            scales = tall(vfac[k * blocks + u])
            weights.append((weight.astype(BF16).astype(F32) * scales).astype(BF16))
        total = own_weight + jnp.sum(added, axis=1, keepdims=True)
        weights = jnp.concatenate(weights, axis=1)
        summed = None
        for r in range(local_rows):
            one = jnp.dot(weights, vc[r, :, at_k], preferred_element_type=F32)
            summed = one if r == 0 else jnp.where(ridx == r, one, summed)
        summed = summed + own_weight.astype(BF16).astype(F32) * new_value
        result = (summed / total).astype(BF16)
        for s in range(per_head):
            asend[k * per_head + s] = result[s * tile:(s + 1) * tile, :]

    def a_copy(o, slot):
        return remote(asend.at[o], abuf.at[slot], a_send.at[o], a_recv.at[slot], o)

    others(lambda o: a_copy(o, me).start())
    abuf[me] = asend[me]
    others(lambda o: q_copy(o, o).wait_send())
    for i in range(wo_parts):
        wo_copy(i).wait()
    others(lambda o: a_copy(o, o).wait_recv())
    pk[...] = abuf[...].astype(F32)
    for j in range(n):
        for g in range(own_heads):
            heads[j * local_rows:(j + 1) * local_rows, g * HD:(g + 1) * HD] = (
                pk[j, g * local_rows:(g + 1) * local_rows, :]
            )
    attended = heads[...].astype(BF16)

    def partial(block):
        start = pl.multiple_of(block * width, width)
        return jnp.dot(attended, wo[:, pl.ds(start, width)], preferred_element_type=F32)

    def core_copy(slot):
        return remote(core_sb.at[slot], core_rb.at[slot], core_send.at[slot], core_recv.at[slot], cpeer)

    def half_of(ref, pos, h):
        return ref.at[pos, pl.ds(h * half_rows, half_rows)]

    def y_copy(pos, h):
        i = 2 * pos + h
        return remote(half_of(y_sb, pos, h), half_of(y_rb, pos, h), y_send.at[i], y_recv.at[i], ypeer)

    def up_copy(pos, h):
        i = 2 * pos + h
        return remote(half_of(z_sb, pos, h), half_of(up_rb, pos, h), z_send.at[i], up_recv.at[i], up)

    def dn_copy(pos, h):
        i = 2 * pos + h
        return remote(half_of(z_sb, pos, h), half_of(dn_rb, pos, h), z_send.at[i], dn_recv.at[i], down)

    def to_core_far(pos):
        core_sb[line + pos] = partial(at(pos, 1 - b, 1 - c)).astype(BF16)
        core_copy(line + pos).start()

    def to_pair(pos):
        term = partial(at(pos, 1 - b, c))
        core_copy(line + pos).wait_recv()
        y_sb[pos] = (term + core_rb[line + pos].astype(F32)).astype(BF16)
        for h in range(2):
            y_copy(pos, h).start()

    def to_core_near(pos):
        core_sb[pos] = partial(at(pos, b, 1 - c)).astype(BF16)
        core_copy(pos).start()

    def to_line(pos):
        term = partial(at(pos, b, c))
        core_copy(pos).wait_recv()
        heads_sum[...] = term + core_rb[pos].astype(F32)
        for h in range(2):
            part = pl.ds(h * half_rows, half_rows)
            y_copy(pos, h).wait_recv()
            heads_sum[part] += y_rb[pos, part].astype(F32)

            @pl.when((pos >= a) & (a > 0))
            def _():
                up_copy(pos, h).wait_recv()
                heads_sum[part] += up_rb[pos, part].astype(F32)

            @pl.when((pos <= a) & (a < line - 1))
            def _():
                dn_copy(pos, h).wait_recv()
                heads_sum[part] += dn_rb[pos, part].astype(F32)

            @pl.when(pos > a)
            def _():
                z_sb[pos, part] = heads_sum[part].astype(BF16)
                up_copy(pos, h).start()

            @pl.when(pos < a)
            def _():
                z_sb[pos, part] = heads_sum[part].astype(BF16)
                dn_copy(pos, h).start()

            @pl.when(pos == a)
            def _():
                out_ref[part] = (x_ref[part].astype(F32) + heads_sum[part]).astype(BF16)

    def far(m):
        return ranked(line - 1 - m)

    to_core_far(far(0))

    def pair_step(m, carry):
        @pl.when(m + 1 < line)
        def _():
            to_core_far(far(m + 1))

        to_pair(far(m))
        return carry
    lax.fori_loop(0, line, pair_step, 0)

    to_core_near(far(0))
    others(lambda o: a_copy(o, o).wait_send())

    def sum_step(m, carry):
        @pl.when(m + 1 < line)
        def _():
            to_core_near(far(m + 1))

        to_line(far(m))
        return carry
    lax.fori_loop(0, line, sum_step, 0)

    def sent_sums(i, carry):
        pos, h = i // 2, i % 2
        y_copy(pos, h).wait_send()

        @pl.when(pos > a)
        def _():
            up_copy(pos, h).wait_send()

        @pl.when(pos < a)
        def _():
            dn_copy(pos, h).wait_send()
        return carry
    lax.fori_loop(0, 2 * line, sent_sums, 0)

    def sent(pos, carry):
        core_copy(pos).wait_send()
        core_copy(line + pos).wait_send()
        return carry
    lax.fori_loop(0, line, sent, 0)


def fused_device(
    n, stream, norm_gain, w_query, w_keyval, w_out, lengths, key_cache, value_cache,
    key_scales, value_scales,
):
    rows, width = stream.shape
    local_rows = lengths.shape[0]
    span = key_cache.shape[1]
    line = n // 4
    qcols = w_query.shape[1]
    tile = (qcols // HD + 1) * local_rows
    vmem = pl.BlockSpec(memory_space=pltpu.VMEM)
    smem = pl.BlockSpec(memory_space=pltpu.SMEM)
    hbm = pl.BlockSpec(memory_space=pl.ANY)
    block = (rows, width)
    dma = pltpu.SemaphoreType.DMA
    return pl.pallas_call(
        functools.partial(fused_kernel, n, rows, width, local_rows, span),
        out_shape=jax.ShapeDtypeStruct(block, BF16),
        in_specs=[smem] * 3 + [hbm] * 7,
        out_specs=vmem,
        scratch_shapes=[
            pltpu.VMEM(block, BF16),
            pltpu.VMEM((1, n * width), F32),
            pltpu.VMEM((8, HD), F32),
            pltpu.VMEM((8, HD), F32),
            pltpu.VMEM((KVH * (span // 128), 8, 128), F32),
            pltpu.VMEM((KVH * (span // 128), 8, 128), F32),
            pltpu.VMEM((n * width, qcols + HD), BF16),
            pltpu.VMEM((HD, n * width), BF16),
            pltpu.VMEM(w_out.shape, BF16),
            pltpu.VMEM(key_cache.shape, BF16),
            pltpu.VMEM(value_cache.shape, BF16),
            pltpu.VMEM((n,) + block, BF16),
            pltpu.VMEM((8, 128), F32),
            pltpu.VMEM((n, 8, 128), F32),
            pltpu.VMEM((rows, qcols + HD), F32),
            pltpu.VMEM((n, tile, HD), F32),
            pltpu.VMEM((n, tile, HD), BF16),
            pltpu.VMEM((n, tile, HD), BF16),
            pltpu.VMEM((n, tile, HD), BF16),
            pltpu.VMEM((n, tile, HD), BF16),
            pltpu.VMEM((rows, qcols), F32),
            pltpu.VMEM((2 * line,) + block, BF16),
            pltpu.VMEM((2 * line,) + block, BF16),
            pltpu.VMEM((line,) + block, BF16),
            pltpu.VMEM((line,) + block, BF16),
            pltpu.VMEM((line,) + block, BF16),
            pltpu.VMEM((line,) + block, BF16),
            pltpu.VMEM((line,) + block, BF16),
            pltpu.VMEM(block, F32),
            dma((n,)), dma((4,)), dma((5,)),
            dma((2 * n,)), dma((2 * line,)), dma((2 * line,)), dma((2 * line,)), dma((4 * line,)),
            dma((n,)), dma((n,)), dma((n,)), dma((n,)), dma((n,)), dma((n,)),
            dma((2 * line,)), dma((2 * line,)), dma((2 * line,)), dma((2 * line,)), dma((2 * line,)),
            dma((2 * line,)), dma((2 * line,)),
        ],
        compiler_params=pltpu.CompilerParams(
            collective_id=0, has_side_effects=True, vmem_limit_bytes=62 * 2**20
        ),
        cost_estimate=pl.CostEstimate(
            flops=4 * rows * w_query.size, bytes_accessed=4 * w_query.size, transcendentals=0
        ),
    )(
        lengths, key_scales, value_scales, stream, norm_gain.reshape(1, -1),
        w_query, w_keyval.T, w_out, key_cache, value_cache,
    )


def per_device(n, *args):
    stream, _, w_query, w_keyval, _, lengths, key_cache, *_ = args
    rows, width = stream.shape
    local_rows = lengths.shape[0]
    qcols, kv_cols = w_query.shape[1], w_keyval.shape[1]
    tiles = (
        n % 4 == 0 and n >= 8 and n % KVH == 0 and width % 128 == 0 and qcols % HD == 0
        and HD % kv_cols == 0 and rows % 32 == 0 and rows <= 128
        and 8 % local_rows == 0
        and (qcols // HD + 1) * local_rows % 16 == 0
        and key_cache.shape[1] // 128 == args[8].shape[1]
    )
    return fused_device(n, *args) if tiles else plain_device(*args)


def solution(mesh):
    return jax.shard_map(
        functools.partial(per_device, mesh.shape["out"]),
        mesh=mesh,
        in_specs=(
            P("groups", "out"),
            P(),
            P(None, "out"),
            P(None, "out"),
            P("out", None),
            P(("groups", "out")),
            P(("groups", "out"), None, None),
            P(("groups", "out"), None, None),
            P(("groups", "out"), None, None),
            P(("groups", "out"), None, None),
        ),
        out_specs=P("groups", "out"),
        check_vma=False,
    )
```

```python
import functools
import math

import jax
import jax.numpy as jnp
from jax import lax
from jax.experimental import pallas as pl
from jax.experimental.pallas import tpu as pltpu
from jax.sharding import PartitionSpec as P

HQ = 48
KVH = 4
HD = 128


rope_base = 1000000.0
norm_eps = 1e-05


def rotate(vec, position):
    half = vec.shape[-1] // 2
    index = jnp.arange(half, dtype=jnp.float32)
    freq = jnp.exp(index * (-2.0 * math.log(rope_base) / vec.shape[-1]))
    angle = position * freq
    cosine = jnp.cos(angle)
    sine = jnp.sin(angle)
    first = vec[..., :half]
    second = vec[..., half:]
    return jnp.concatenate(
        [first * cosine - second * sine, second * cosine + first * sine], axis=-1
    )


def dequant(cache, scales):
    rows, span, width = cache.shape
    blocks = scales.shape[1]
    factor = jnp.exp2(scales.astype(jnp.float32)).astype(jnp.bfloat16)
    shaped = cache.reshape(rows, blocks, span // blocks, KVH, width // KVH)
    return (shaped * factor[:, :, None, :, None]).reshape(rows, span, KVH, width // KVH)


def plain_device(
    stream,
    norm_gain,
    w_query,
    w_keyval,
    w_out,
    lengths,
    key_cache,
    value_cache,
    key_scales,
    value_scales,
):
    local_rows = lengths.shape[0]
    xf = stream.astype(jnp.float32)
    whole = lax.all_gather(stream, "out", axis=1, tiled=True).astype(jnp.float32)
    meansq = jnp.mean(whole * whole, axis=-1, keepdims=True)
    normed = (whole * lax.rsqrt(meansq + norm_eps) * norm_gain).astype(jnp.bfloat16)
    q_local = jnp.dot(normed, w_query, preferred_element_type=jnp.float32).astype(jnp.bfloat16)
    kv_local = jnp.dot(normed, w_keyval, preferred_element_type=jnp.float32).astype(jnp.bfloat16)
    q_rows, kv_rows = (
        lax.all_to_all(q_local, "out", split_axis=0, concat_axis=1, tiled=True),
        lax.all_to_all(kv_local, "out", split_axis=0, concat_axis=1, tiled=True),
    )
    position = lengths.astype(jnp.float32)[:, None, None]
    rotated = rotate(q_rows.astype(jnp.float32).reshape(local_rows, HQ, HD), position).astype(
        jnp.bfloat16
    )
    rotated = rotated.reshape(local_rows, KVH, HQ // KVH, HD)
    new_key = rotate(
        kv_rows[:, : KVH * HD].astype(jnp.float32).reshape(local_rows, KVH, HD), position
    ).astype(jnp.bfloat16)
    new_value = kv_rows[:, KVH * HD :].reshape(local_rows, KVH, HD)
    factor = HD ** (-0.5)
    own = jnp.einsum("rkgd,rkd->rkg", rotated, new_key, preferred_element_type=jnp.float32) * factor
    span = key_cache.shape[1]
    scores = (
        jnp.einsum(
            "rkgd,rjkd->rkgj",
            rotated,
            dequant(key_cache, key_scales),
            preferred_element_type=jnp.float32,
        )
        * factor
    )
    valid = jnp.arange(span, dtype=jnp.int32)[None, :] < lengths[:, None]
    scores = jnp.where(valid[:, None, None, :], scores, -jnp.inf)
    top = jnp.maximum(jnp.max(scores, axis=-1), own)
    weights = jnp.exp(scores - top[..., None])
    own_weight = jnp.exp(own - top)
    total = jnp.sum(weights, axis=-1) + own_weight
    own_rounded = lax.optimization_barrier(own_weight.astype(jnp.bfloat16)).astype(jnp.float32)
    summed = jnp.einsum(
        "rkgj,rjkd->rkgd",
        weights.astype(jnp.bfloat16),
        dequant(value_cache, value_scales),
        preferred_element_type=jnp.float32,
    )
    summed = summed + own_rounded[..., None] * new_value.astype(jnp.float32)[:, :, None, :]
    attended = (summed / total[..., None]).astype(jnp.bfloat16).reshape(local_rows, HQ * HD)
    heads = lax.all_to_all(attended, "out", split_axis=1, concat_axis=0, tiled=True)
    partial_terms = jnp.dot(heads, w_out, preferred_element_type=jnp.float32)
    projected = lax.psum_scatter(partial_terms, "out", scatter_dimension=1, tiled=True)
    return (xf + projected).astype(jnp.bfloat16)


MESH = pl.DeviceIdType.MESH
F32 = jnp.float32
BF16 = jnp.bfloat16
CONTRACT_LAST = (((1,), (1,)), ((), ()))


def fused_kernel(
    n, rows, width, local_rows, span,
    len_ref, ks_ref, vs_ref,
    x_hbm, gain_hbm, wq_hbm, wkv_hbm, wo_hbm, kc_hbm, vc_hbm,
    out_ref,
    x_ref, gain_ref, cos_ref, sin_ref, kfac, vfac, wq, wkv, wo, kc, vc, xbuf, ssend, sbuf, accq, pk, qsend, qbuf, asend, abuf, heads,
    core_sb, core_rb, y_sb, y_rb, z_sb, up_rb, dn_rb, heads_sum,
    wq_sem, wo_sem, w_sem,
    ag_recv, ag_up, ag_dn, ag_y, ag_core,
    ss_send, ss_recv, q_send, q_recv, a_send, a_recv,
    core_send, core_recv, y_send, y_recv, z_send, up_recv, dn_recv,
):
    line = n // 4
    qcols = heads.shape[1]
    kv_cols = wkv_hbm.shape[0]
    own_heads = qcols // HD
    tile = qbuf.shape[1]
    per_head = n // KVH
    qrows = per_head * tile
    me = lax.axis_index("out")
    grp = lax.axis_index("groups")
    a = me // 4
    b = (me // 2) % 2
    c = me % 2

    def at(pos, bb, cc):
        return (pos * 2 + bb) * 2 + cc

    up, down = at(a + 1, b, c), at(a - 1, b, c)
    ypeer, cpeer = at(a, 1 - b, c), at(a, b, 1 - c)
    low, high = a, line - 1 - a
    least = jnp.minimum(low, high)

    def ranked(m):
        d = (m + 1) // 2
        near = jnp.where(m % 2 == 1, a - d, a + d)
        far = jnp.where(high > low, a + (m - least), a - (m - least))
        return jnp.where(m <= 2 * least, near, far)

    def remote(src, dst, ssem, rsem, to):
        return pltpu.make_async_remote_copy(
            src_ref=src, dst_ref=dst, send_sem=ssem, recv_sem=rsem,
            device_id=(grp, to), device_id_type=MESH,
        )

    def wq_copy(i):
        at_rows = pl.ds(pl.multiple_of(i * width, width), width)
        return pltpu.make_async_copy(wq_hbm.at[at_rows], wq.at[at_rows, pl.ds(0, qcols)], wq_sem.at[i])

    wo_parts = wo_sem.shape[0]
    wo_rows = wo.shape[0] // wo_parts

    def wo_copy(i):
        at_rows = pl.ds(i * wo_rows, wo_rows)
        return pltpu.make_async_copy(wo_hbm.at[at_rows], wo.at[at_rows], wo_sem.at[i])

    wkv_copy = pltpu.make_async_copy(wkv_hbm, wkv.at[pl.ds(0, kv_cols)], w_sem.at[0])
    kc_copy = pltpu.make_async_copy(kc_hbm, kc, w_sem.at[1])
    vc_copy = pltpu.make_async_copy(vc_hbm, vc, w_sem.at[2])

    x_copy = pltpu.make_async_copy(x_hbm, x_ref, w_sem.at[3])
    gain_copy = pltpu.make_async_copy(gain_hbm, gain_ref, w_sem.at[4])
    x_copy.start()
    gain_copy.start()

    barrier = pltpu.get_barrier_semaphore()

    def others(body):
        def step(i, carry):
            body(lax.rem(me + i, n))
            return carry
        lax.fori_loop(1, n, step, 0)

    others(lambda o: pl.semaphore_signal(barrier, inc=1, device_id=(grp, o), device_id_type=MESH))

    wkv_copy.start()
    if kv_cols < HD:
        wkv[kv_cols:, :] = jnp.zeros((HD - kv_cols, n * width), BF16)

    def start_wq(m, carry):
        pos = ranked(m)
        for bb, cc in ((b, c), (b, 1 - c), (1 - b, c), (1 - b, 1 - c)):
            wq_copy(at(pos, bb, cc)).start()
        return carry
    lax.fori_loop(0, line, start_wq, 0)

    x_copy.wait()
    xbuf[me] = x_ref[...]
    xf = x_ref[...].astype(F32)
    square = jnp.sum(xf * xf, axis=1, keepdims=True)
    spread = jnp.transpose(jnp.broadcast_to(square, (rows, 128)))
    ssend[...] = jnp.zeros_like(ssend)
    ssend[:, 0:rows] = spread[0:8, :]
    sbuf[me] = ssend[...]
    accq[...] = jnp.zeros_like(accq)

    pl.semaphore_wait(barrier, n - 1)

    half_rows = rows // 2

    def ag_copy(block, h, ssem, to):
        part = xbuf.at[block, pl.ds(h * half_rows, half_rows)]
        return remote(part, part, ssem, ag_recv.at[2 * block + h], to)

    def ag_wait(block, h):
        ag_copy(block, h, ag_core.at[0], cpeer).wait_recv()

    def spread_line(pos, h):
        block = at(pos, b, c)

        @pl.when((pos <= a) & (a < line - 1))
        def _():
            ag_copy(block, h, ag_up.at[2 * pos + h], up).start()

        @pl.when((pos >= a) & (a > 0))
        def _():
            ag_copy(block, h, ag_dn.at[2 * pos + h], down).start()

        ag_copy(block, h, ag_y.at[2 * pos + h], ypeer).start()
        ag_copy(block, h, ag_core.at[2 * pos + h], cpeer).start()

    def ss_copy(o, slot):
        return remote(ssend, sbuf.at[slot], ss_send.at[o], ss_recv.at[slot], o)

    others(lambda o: ss_copy(o, me).start())
    for h in range(2):
        spread_line(a, h)
    ridx = lax.broadcasted_iota(jnp.int32, (qrows, 128), 0) % local_rows
    pick = lax.broadcasted_iota(jnp.int32, (qrows, tile), 0) % local_rows
    pick = pick + own_heads * local_rows == lax.broadcasted_iota(jnp.int32, (qrows, tile), 1)
    pick = pick.astype(F32).astype(BF16)
    blocks = span // 128
    few = lax.broadcasted_iota(jnp.int32, (8, 128), 0) % local_rows
    lane8 = lax.broadcasted_iota(jnp.int32, (8, 128), 1)

    def by_row(values):
        res = jnp.full((8, 128), values[0])
        for r in range(1, local_rows):
            res = jnp.where(few == r, values[r], res)
        return res

    def tall(v):
        return jnp.concatenate([v] * (qrows // 8), axis=0)

    limit8 = by_row([len_ref[r] for r in range(local_rows)])
    freq = jnp.exp((lane8 % (HD // 2)).astype(F32) * (-2.0 * math.log(rope_base) / HD))
    angle = limit8.astype(F32) * freq
    cos_ref[...] = jnp.cos(angle)
    sin_ref[...] = jnp.where(lane8 < HD // 2, -1.0, 1.0) * jnp.sin(angle)
    for k in range(KVH):
        for u in range(blocks):
            for ref, table in ((ks_ref, kfac), (vs_ref, vfac)):
                power = by_row([ref[r, u, k] for r in range(local_rows)]).astype(F32)
                table[k * blocks + u] = jnp.exp2(power).astype(BF16).astype(F32)

    def take_line(m, h):
        @pl.when(m < line)
        def _():
            pos = ranked(m)
            ag_wait(at(pos, b, c), h)
            spread_line(pos, h)

    def take_pair(m, h):
        @pl.when(m < line)
        def _():
            pos = ranked(m)
            block = at(pos, 1 - b, c)
            ag_wait(block, h)
            ag_copy(block, h, ag_core.at[2 * (line + pos) + h], cpeer).start()

    for h in range(2):
        take_line(1, h)
        take_pair(0, h)

    wkv_copy.wait()

    def turn(i, carry):
        start = pl.multiple_of(i * width, width)
        turned = jnp.transpose(wkv[:, pl.ds(start, width)].astype(F32)).astype(BF16)
        wq[pl.ds(start, width), qcols:] = turned
        return carry
    lax.fori_loop(0, n, turn, 0)
    others(lambda o: ss_copy(o, o).wait_recv())
    total_sq = jnp.sum(sbuf[...], axis=0)[0:1, :]
    column = jnp.transpose(jnp.broadcast_to(total_sq, (128, 128)))[0:rows, 0:1]
    scale = lax.rsqrt(column * (1.0 / (n * width)) + norm_eps)
    gain_copy.wait()

    def project(block):
        wq_copy(block).wait()
        start = pl.multiple_of(block * width, width)
        normed = (xbuf[block].astype(F32) * scale * gain_ref[:, pl.ds(start, width)]).astype(BF16)
        accq[...] += jnp.dot(normed, wq[pl.ds(start, width), :], preferred_element_type=F32)

    def gather_step(m, carry):
        prev = ranked(m - 1)
        project(at(prev, b, c))
        take_line(m + 1, 0)
        take_pair(m, 0)
        cblock = at(prev, b, 1 - c)
        for h in range(2):
            ag_wait(cblock, h)
        project(cblock)
        take_line(m + 1, 1)
        take_pair(m, 1)
        project(at(prev, 1 - b, c))

        @pl.when(m > 1)
        def _():
            block = at(ranked(m - 2), 1 - b, 1 - c)
            for h in range(2):
                ag_wait(block, h)
            project(block)

        @pl.when(m == 1)
        def _():
            kc_copy.start()
            vc_copy.start()
            for i in range(wo_parts):
                wo_copy(i).start()
        return carry
    lax.fori_loop(1, line + 1, gather_step, 0)
    last = at(ranked(line - 1), 1 - b, 1 - c)
    for h in range(2):
        ag_wait(last, h)
    project(last)

    def q_copy(o, slot):
        return remote(qsend.at[o], qbuf.at[slot], q_send.at[o], q_recv.at[slot], o)

    pk[...] = jnp.zeros_like(pk)
    q_all = accq[...]
    kv_all = q_all[:, qcols:qcols + kv_cols]
    for j in range(n):
        mine = slice(j * local_rows, (j + 1) * local_rows)
        for g in range(own_heads):
            pk[j, g * local_rows:(g + 1) * local_rows, :] = q_all[mine, g * HD:(g + 1) * HD]
        pk[j, own_heads * local_rows:tile, 0:kv_cols] = kv_all[mine, :]
        qsend[j] = pk[j].astype(BF16)

        @pl.when(j != me)
        def _():
            q_copy(j, me).start()

    qbuf[me] = qsend[me]
    def sent_gather(i, carry):
        pos, h = i // 2, i % 2
        block = at(pos, b, c)

        @pl.when((pos <= a) & (a < line - 1))
        def _():
            ag_copy(block, h, ag_up.at[2 * pos + h], up).wait_send()

        @pl.when((pos >= a) & (a > 0))
        def _():
            ag_copy(block, h, ag_dn.at[2 * pos + h], down).wait_send()

        ag_copy(block, h, ag_y.at[2 * pos + h], ypeer).wait_send()
        ag_copy(block, h, ag_core.at[2 * pos + h], cpeer).wait_send()
        ag_copy(at(pos, 1 - b, c), h, ag_core.at[2 * (line + pos) + h], cpeer).wait_send()
        return carry
    lax.fori_loop(0, 2 * line, sent_gather, 0)
    others(lambda o: ss_copy(o, o).wait_send())


    limit = tall(limit8)
    lane = lax.broadcasted_iota(jnp.int32, (qrows, 128), 1)
    cosine, sine = tall(cos_ref[...]), tall(sin_ref[...])

    def rotated(v):
        return (v * cosine + pltpu.roll(v, HD // 2, 1) * sine).astype(BF16)

    kc_copy.wait()
    vc_copy.wait()
    others(lambda o: q_copy(o, o).wait_recv())

    pieces = HD // kv_cols
    factor = HD ** (-0.5)

    def new_head(first):
        res = None
        for p in range(pieces):
            part = jnp.dot(pick, qbuf[first + p], preferred_element_type=F32)
            part = part if p == 0 else pltpu.roll(part, p * kv_cols, 1)
            res = part if res is None else res + part
        return res

    def a_copy(o, slot):
        return remote(asend.at[o], abuf.at[slot], a_send.at[o], a_recv.at[slot], o)

    for k in range(KVH):
        at_k = slice(k * HD, (k + 1) * HD)
        query = rotated(qbuf[k * per_head:(k + 1) * per_head].astype(F32).reshape(qrows, HD))
        new_key = rotated(new_head(k * pieces)).astype(F32)
        new_value = new_head((KVH + k) * pieces)
        own = jnp.sum(query.astype(F32) * new_key, axis=1, keepdims=True) * factor
        score = None
        for r in range(local_rows):
            one = lax.dot_general(query, kc[r, :, at_k], CONTRACT_LAST, preferred_element_type=F32)
            cut = [one[:, 128 * u:128 * (u + 1)] for u in range(blocks)]
            score = cut if r == 0 else [jnp.where(ridx == r, x, y) for x, y in zip(cut, score)]
        highest = None
        for u in range(blocks):
            scales = tall(kfac[k * blocks + u])
            score[u] = jnp.where(lane + 128 * u < limit, score[u] * scales * factor, -jnp.inf)
            highest = score[u] if u == 0 else jnp.maximum(highest, score[u])
        top = jnp.maximum(own, jnp.max(highest, axis=1, keepdims=True))
        own_weight = jnp.exp(own - top)
        added = None
        weights = []
        for u in range(blocks):
            weight = jnp.exp(score[u] - top)
            added = weight if u == 0 else added + weight
            scales = tall(vfac[k * blocks + u])
            weights.append((weight.astype(BF16).astype(F32) * scales).astype(BF16))
        total = own_weight + jnp.sum(added, axis=1, keepdims=True)
        weights = jnp.concatenate(weights, axis=1)
        summed = None
        for r in range(local_rows):
            one = jnp.dot(weights, vc[r, :, at_k], preferred_element_type=F32)
            summed = one if r == 0 else jnp.where(ridx == r, one, summed)
        summed = summed + own_weight.astype(BF16).astype(F32) * new_value
        result = (summed / total).astype(BF16)
        for s in range(per_head):
            o = k * per_head + s
            asend[o] = result[s * tile:(s + 1) * tile, :]

            @pl.when(o != me)
            def _():
                a_copy(o, me).start()

    abuf[me] = asend[me]
    others(lambda o: q_copy(o, o).wait_send())
    for i in range(wo_parts):
        wo_copy(i).wait()
    others(lambda o: a_copy(o, o).wait_recv())
    pk[...] = abuf[...].astype(F32)
    for j in range(n):
        for g in range(own_heads):
            heads[j * local_rows:(j + 1) * local_rows, g * HD:(g + 1) * HD] = (
                pk[j, g * local_rows:(g + 1) * local_rows, :]
            )
    attended = heads[...].astype(BF16)

    def partial(block):
        start = pl.multiple_of(block * width, width)
        return jnp.dot(attended, wo[:, pl.ds(start, width)], preferred_element_type=F32)

    def core_copy(slot):
        return remote(core_sb.at[slot], core_rb.at[slot], core_send.at[slot], core_recv.at[slot], cpeer)

    def half_of(ref, pos, h):
        return ref.at[pos, pl.ds(h * half_rows, half_rows)]

    def y_copy(pos, h):
        i = 2 * pos + h
        return remote(half_of(y_sb, pos, h), half_of(y_rb, pos, h), y_send.at[i], y_recv.at[i], ypeer)

    def up_copy(pos, h):
        i = 2 * pos + h
        return remote(half_of(z_sb, pos, h), half_of(up_rb, pos, h), z_send.at[i], up_recv.at[i], up)

    def dn_copy(pos, h):
        i = 2 * pos + h
        return remote(half_of(z_sb, pos, h), half_of(dn_rb, pos, h), z_send.at[i], dn_recv.at[i], down)

    def to_core_far(pos):
        core_sb[line + pos] = partial(at(pos, 1 - b, 1 - c)).astype(BF16)
        core_copy(line + pos).start()

    def to_pair(pos):
        term = partial(at(pos, 1 - b, c))
        core_copy(line + pos).wait_recv()
        y_sb[pos] = (term + core_rb[line + pos].astype(F32)).astype(BF16)
        for h in range(2):
            y_copy(pos, h).start()

    def to_core_near(pos):
        core_sb[pos] = partial(at(pos, b, 1 - c)).astype(BF16)
        core_copy(pos).start()

    def to_line(pos):
        term = partial(at(pos, b, c))
        core_copy(pos).wait_recv()
        heads_sum[...] = term + core_rb[pos].astype(F32)
        for h in range(2):
            part = pl.ds(h * half_rows, half_rows)
            y_copy(pos, h).wait_recv()
            heads_sum[part] += y_rb[pos, part].astype(F32)

            @pl.when((pos >= a) & (a > 0))
            def _():
                up_copy(pos, h).wait_recv()
                heads_sum[part] += up_rb[pos, part].astype(F32)

            @pl.when((pos <= a) & (a < line - 1))
            def _():
                dn_copy(pos, h).wait_recv()
                heads_sum[part] += dn_rb[pos, part].astype(F32)

            @pl.when(pos > a)
            def _():
                z_sb[pos, part] = heads_sum[part].astype(BF16)
                up_copy(pos, h).start()

            @pl.when(pos < a)
            def _():
                z_sb[pos, part] = heads_sum[part].astype(BF16)
                dn_copy(pos, h).start()

            @pl.when(pos == a)
            def _():
                out_ref[part] = (x_ref[part].astype(F32) + heads_sum[part]).astype(BF16)

    def far(m):
        return ranked(line - 1 - m)

    to_core_far(far(0))

    def pair_step(m, carry):
        @pl.when(m + 1 < line)
        def _():
            to_core_far(far(m + 1))

        to_pair(far(m))
        return carry
    lax.fori_loop(0, line, pair_step, 0)

    to_core_near(far(0))
    others(lambda o: a_copy(o, o).wait_send())

    def sum_step(m, carry):
        @pl.when(m + 1 < line)
        def _():
            to_core_near(far(m + 1))

        to_line(far(m))
        return carry
    lax.fori_loop(0, line, sum_step, 0)

    def sent_sums(i, carry):
        pos, h = i // 2, i % 2
        y_copy(pos, h).wait_send()

        @pl.when(pos > a)
        def _():
            up_copy(pos, h).wait_send()

        @pl.when(pos < a)
        def _():
            dn_copy(pos, h).wait_send()
        return carry
    lax.fori_loop(0, 2 * line, sent_sums, 0)

    def sent(pos, carry):
        core_copy(pos).wait_send()
        core_copy(line + pos).wait_send()
        return carry
    lax.fori_loop(0, line, sent, 0)


def fused_device(
    n, stream, norm_gain, w_query, w_keyval, w_out, lengths, key_cache, value_cache,
    key_scales, value_scales,
):
    rows, width = stream.shape
    local_rows = lengths.shape[0]
    span = key_cache.shape[1]
    line = n // 4
    qcols = w_query.shape[1]
    tile = (qcols // HD + 1) * local_rows
    vmem = pl.BlockSpec(memory_space=pltpu.VMEM)
    smem = pl.BlockSpec(memory_space=pltpu.SMEM)
    hbm = pl.BlockSpec(memory_space=pl.ANY)
    block = (rows, width)
    dma = pltpu.SemaphoreType.DMA
    return pl.pallas_call(
        functools.partial(fused_kernel, n, rows, width, local_rows, span),
        out_shape=jax.ShapeDtypeStruct(block, BF16),
        in_specs=[smem] * 3 + [hbm] * 7,
        out_specs=vmem,
        scratch_shapes=[
            pltpu.VMEM(block, BF16),
            pltpu.VMEM((1, n * width), F32),
            pltpu.VMEM((8, HD), F32),
            pltpu.VMEM((8, HD), F32),
            pltpu.VMEM((KVH * (span // 128), 8, 128), F32),
            pltpu.VMEM((KVH * (span // 128), 8, 128), F32),
            pltpu.VMEM((n * width, qcols + HD), BF16),
            pltpu.VMEM((HD, n * width), BF16),
            pltpu.VMEM(w_out.shape, BF16),
            pltpu.VMEM(key_cache.shape, BF16),
            pltpu.VMEM(value_cache.shape, BF16),
            pltpu.VMEM((n,) + block, BF16),
            pltpu.VMEM((8, 128), F32),
            pltpu.VMEM((n, 8, 128), F32),
            pltpu.VMEM((rows, qcols + HD), F32),
            pltpu.VMEM((n, tile, HD), F32),
            pltpu.VMEM((n, tile, HD), BF16),
            pltpu.VMEM((n, tile, HD), BF16),
            pltpu.VMEM((n, tile, HD), BF16),
            pltpu.VMEM((n, tile, HD), BF16),
            pltpu.VMEM((rows, qcols), F32),
            pltpu.VMEM((2 * line,) + block, BF16),
            pltpu.VMEM((2 * line,) + block, BF16),
            pltpu.VMEM((line,) + block, BF16),
            pltpu.VMEM((line,) + block, BF16),
            pltpu.VMEM((line,) + block, BF16),
            pltpu.VMEM((line,) + block, BF16),
            pltpu.VMEM((line,) + block, BF16),
            pltpu.VMEM(block, F32),
            dma((n,)), dma((4,)), dma((5,)),
            dma((2 * n,)), dma((2 * line,)), dma((2 * line,)), dma((2 * line,)), dma((4 * line,)),
            dma((n,)), dma((n,)), dma((n,)), dma((n,)), dma((n,)), dma((n,)),
            dma((2 * line,)), dma((2 * line,)), dma((2 * line,)), dma((2 * line,)), dma((2 * line,)),
            dma((2 * line,)), dma((2 * line,)),
        ],
        compiler_params=pltpu.CompilerParams(
            collective_id=0, has_side_effects=True, vmem_limit_bytes=62 * 2**20
        ),
        cost_estimate=pl.CostEstimate(
            flops=4 * rows * w_query.size, bytes_accessed=4 * w_query.size, transcendentals=0
        ),
    )(
        lengths, key_scales, value_scales, stream, norm_gain.reshape(1, -1),
        w_query, w_keyval.T, w_out, key_cache, value_cache,
    )


def per_device(n, *args):
    stream, _, w_query, w_keyval, _, lengths, key_cache, *_ = args
    rows, width = stream.shape
    local_rows = lengths.shape[0]
    qcols, kv_cols = w_query.shape[1], w_keyval.shape[1]
    tiles = (
        n % 4 == 0 and n >= 8 and n % KVH == 0 and width % 128 == 0 and qcols % HD == 0
        and HD % kv_cols == 0 and rows % 32 == 0 and rows <= 128
        and 8 % local_rows == 0
        and (qcols // HD + 1) * local_rows % 16 == 0
        and key_cache.shape[1] // 128 == args[8].shape[1]
    )
    return fused_device(n, *args) if tiles else plain_device(*args)


def solution(mesh):
    return jax.shard_map(
        functools.partial(per_device, mesh.shape["out"]),
        mesh=mesh,
        in_specs=(
            P("groups", "out"),
            P(),
            P(None, "out"),
            P(None, "out"),
            P("out", None),
            P(("groups", "out")),
            P(("groups", "out"), None, None),
            P(("groups", "out"), None, None),
            P(("groups", "out"), None, None),
            P(("groups", "out"), None, None),
        ),
        out_specs=P("groups", "out"),
        check_vma=False,
    )
```

```python
import functools
import math

import jax
import jax.numpy as jnp
from jax import lax
from jax.experimental import pallas as pl
from jax.experimental.pallas import tpu as pltpu
from jax.sharding import PartitionSpec as P

HQ = 48
KVH = 4
HD = 128


rope_base = 1000000.0
norm_eps = 1e-05


def rotate(vec, position):
    half = vec.shape[-1] // 2
    index = jnp.arange(half, dtype=jnp.float32)
    freq = jnp.exp(index * (-2.0 * math.log(rope_base) / vec.shape[-1]))
    angle = position * freq
    cosine = jnp.cos(angle)
    sine = jnp.sin(angle)
    first = vec[..., :half]
    second = vec[..., half:]
    return jnp.concatenate(
        [first * cosine - second * sine, second * cosine + first * sine], axis=-1
    )


def dequant(cache, scales):
    rows, span, width = cache.shape
    blocks = scales.shape[1]
    factor = jnp.exp2(scales.astype(jnp.float32)).astype(jnp.bfloat16)
    shaped = cache.reshape(rows, blocks, span // blocks, KVH, width // KVH)
    return (shaped * factor[:, :, None, :, None]).reshape(rows, span, KVH, width // KVH)


def plain_device(
    stream,
    norm_gain,
    w_query,
    w_keyval,
    w_out,
    lengths,
    key_cache,
    value_cache,
    key_scales,
    value_scales,
):
    local_rows = lengths.shape[0]
    xf = stream.astype(jnp.float32)
    whole = lax.all_gather(stream, "out", axis=1, tiled=True).astype(jnp.float32)
    meansq = jnp.mean(whole * whole, axis=-1, keepdims=True)
    normed = (whole * lax.rsqrt(meansq + norm_eps) * norm_gain).astype(jnp.bfloat16)
    q_local = jnp.dot(normed, w_query, preferred_element_type=jnp.float32).astype(jnp.bfloat16)
    kv_local = jnp.dot(normed, w_keyval, preferred_element_type=jnp.float32).astype(jnp.bfloat16)
    q_rows, kv_rows = (
        lax.all_to_all(q_local, "out", split_axis=0, concat_axis=1, tiled=True),
        lax.all_to_all(kv_local, "out", split_axis=0, concat_axis=1, tiled=True),
    )
    position = lengths.astype(jnp.float32)[:, None, None]
    rotated = rotate(q_rows.astype(jnp.float32).reshape(local_rows, HQ, HD), position).astype(
        jnp.bfloat16
    )
    rotated = rotated.reshape(local_rows, KVH, HQ // KVH, HD)
    new_key = rotate(
        kv_rows[:, : KVH * HD].astype(jnp.float32).reshape(local_rows, KVH, HD), position
    ).astype(jnp.bfloat16)
    new_value = kv_rows[:, KVH * HD :].reshape(local_rows, KVH, HD)
    factor = HD ** (-0.5)
    own = jnp.einsum("rkgd,rkd->rkg", rotated, new_key, preferred_element_type=jnp.float32) * factor
    span = key_cache.shape[1]
    scores = (
        jnp.einsum(
            "rkgd,rjkd->rkgj",
            rotated,
            dequant(key_cache, key_scales),
            preferred_element_type=jnp.float32,
        )
        * factor
    )
    valid = jnp.arange(span, dtype=jnp.int32)[None, :] < lengths[:, None]
    scores = jnp.where(valid[:, None, None, :], scores, -jnp.inf)
    top = jnp.maximum(jnp.max(scores, axis=-1), own)
    weights = jnp.exp(scores - top[..., None])
    own_weight = jnp.exp(own - top)
    total = jnp.sum(weights, axis=-1) + own_weight
    own_rounded = lax.optimization_barrier(own_weight.astype(jnp.bfloat16)).astype(jnp.float32)
    summed = jnp.einsum(
        "rkgj,rjkd->rkgd",
        weights.astype(jnp.bfloat16),
        dequant(value_cache, value_scales),
        preferred_element_type=jnp.float32,
    )
    summed = summed + own_rounded[..., None] * new_value.astype(jnp.float32)[:, :, None, :]
    attended = (summed / total[..., None]).astype(jnp.bfloat16).reshape(local_rows, HQ * HD)
    heads = lax.all_to_all(attended, "out", split_axis=1, concat_axis=0, tiled=True)
    partial_terms = jnp.dot(heads, w_out, preferred_element_type=jnp.float32)
    projected = lax.psum_scatter(partial_terms, "out", scatter_dimension=1, tiled=True)
    return (xf + projected).astype(jnp.bfloat16)


MESH = pl.DeviceIdType.MESH
F32 = jnp.float32
BF16 = jnp.bfloat16
CONTRACT_LAST = (((1,), (1,)), ((), ()))


def fused_kernel(
    n, rows, width, local_rows, span,
    len_ref, ks_ref, vs_ref,
    x_hbm, gain_hbm, wq_hbm, wkv_hbm, wo_hbm, kc_hbm, vc_hbm,
    out_ref,
    x_ref, gain_ref, cos_ref, sin_ref, kfac, vfac, wq, wkv, wo, kc, vc, xbuf, ssend, sbuf, accq, pk, qsend, qbuf, asend, abuf, heads,
    core_sb, core_rb, y_sb, y_rb, z_sb, up_rb, dn_rb, heads_sum,
    wq_sem, wo_sem, w_sem,
    ag_recv, ag_up, ag_dn, ag_y, ag_core,
    ss_send, ss_recv, q_send, q_recv, a_send, a_recv,
    core_send, core_recv, y_send, y_recv, z_send, up_recv, dn_recv,
):
    line = n // 4
    qcols = heads.shape[1]
    kv_cols = wkv_hbm.shape[0]
    own_heads = qcols // HD
    tile = qbuf.shape[1]
    per_head = n // KVH
    qrows = per_head * tile
    me = lax.axis_index("out")
    grp = lax.axis_index("groups")
    a = me // 4
    b = (me // 2) % 2
    c = me % 2

    def at(pos, bb, cc):
        return (pos * 2 + bb) * 2 + cc

    up, down = at(a + 1, b, c), at(a - 1, b, c)
    ypeer, cpeer = at(a, 1 - b, c), at(a, b, 1 - c)
    low, high = a, line - 1 - a
    least = jnp.minimum(low, high)

    def ranked(m):
        d = (m + 1) // 2
        near = jnp.where(m % 2 == 1, a - d, a + d)
        far = jnp.where(high > low, a + (m - least), a - (m - least))
        return jnp.where(m <= 2 * least, near, far)

    def remote(src, dst, ssem, rsem, to):
        return pltpu.make_async_remote_copy(
            src_ref=src, dst_ref=dst, send_sem=ssem, recv_sem=rsem,
            device_id=(grp, to), device_id_type=MESH,
        )

    def wq_copy(i):
        at_rows = pl.ds(pl.multiple_of(i * width, width), width)
        return pltpu.make_async_copy(wq_hbm.at[at_rows], wq.at[at_rows, pl.ds(0, qcols)], wq_sem.at[i])

    wo_parts = wo_sem.shape[0]
    wo_rows = wo.shape[0] // wo_parts

    def wo_copy(i):
        at_rows = pl.ds(i * wo_rows, wo_rows)
        return pltpu.make_async_copy(wo_hbm.at[at_rows], wo.at[at_rows], wo_sem.at[i])

    wkv_copy = pltpu.make_async_copy(wkv_hbm, wkv.at[pl.ds(0, kv_cols)], w_sem.at[0])
    kc_copy = pltpu.make_async_copy(kc_hbm, kc, w_sem.at[1])
    vc_copy = pltpu.make_async_copy(vc_hbm, vc, w_sem.at[2])

    x_copy = pltpu.make_async_copy(x_hbm, x_ref, w_sem.at[3])
    gain_copy = pltpu.make_async_copy(gain_hbm, gain_ref, w_sem.at[4])
    x_copy.start()
    gain_copy.start()

    barrier = pltpu.get_barrier_semaphore()

    def others(body):
        def step(i, carry):
            body(lax.rem(me + i, n))
            return carry
        lax.fori_loop(1, n, step, 0)

    others(lambda o: pl.semaphore_signal(barrier, inc=1, device_id=(grp, o), device_id_type=MESH))

    wkv_copy.start()
    if kv_cols < HD:
        wkv[kv_cols:, :] = jnp.zeros((HD - kv_cols, n * width), BF16)

    def start_wq(m, carry):
        pos = ranked(m)
        for bb, cc in ((b, c), (b, 1 - c), (1 - b, c), (1 - b, 1 - c)):
            wq_copy(at(pos, bb, cc)).start()
        return carry
    lax.fori_loop(0, line, start_wq, 0)

    x_copy.wait()
    xbuf[me] = x_ref[...]
    xf = x_ref[...].astype(F32)
    square = jnp.sum(xf * xf, axis=1, keepdims=True)
    spread = jnp.transpose(jnp.broadcast_to(square, (rows, 128)))
    ssend[...] = jnp.zeros_like(ssend)
    ssend[:, 0:rows] = spread[0:8, :]
    sbuf[me] = ssend[...]
    accq[...] = jnp.zeros_like(accq)

    pl.semaphore_wait(barrier, n - 1)

    half_rows = rows // 2

    def ag_copy(block, h, ssem, to):
        part = xbuf.at[block, pl.ds(h * half_rows, half_rows)]
        return remote(part, part, ssem, ag_recv.at[2 * block + h], to)

    def ag_wait(block, h):
        ag_copy(block, h, ag_core.at[0], cpeer).wait_recv()

    def spread_line(pos, h):
        block = at(pos, b, c)
        ag_copy(block, h, ag_y.at[2 * pos + h], ypeer).start()

        @pl.when((pos <= a) & (a < line - 1))
        def _():
            ag_copy(block, h, ag_up.at[2 * pos + h], up).start()

        @pl.when((pos >= a) & (a > 0))
        def _():
            ag_copy(block, h, ag_dn.at[2 * pos + h], down).start()

        ag_copy(block, h, ag_core.at[2 * pos + h], cpeer).start()

    def ss_copy(o, slot):
        return remote(ssend, sbuf.at[slot], ss_send.at[o], ss_recv.at[slot], o)

    for h in range(2):
        spread_line(a, h)
    others(lambda o: ss_copy(o, me).start())
    ridx = lax.broadcasted_iota(jnp.int32, (qrows, 128), 0) % local_rows
    pick = lax.broadcasted_iota(jnp.int32, (qrows, tile), 0) % local_rows
    pick = pick + own_heads * local_rows == lax.broadcasted_iota(jnp.int32, (qrows, tile), 1)
    pick = pick.astype(F32).astype(BF16)
    blocks = span // 128
    few = lax.broadcasted_iota(jnp.int32, (8, 128), 0) % local_rows
    lane8 = lax.broadcasted_iota(jnp.int32, (8, 128), 1)

    def by_row(values):
        res = jnp.full((8, 128), values[0])
        for r in range(1, local_rows):
            res = jnp.where(few == r, values[r], res)
        return res

    def tall(v):
        return jnp.concatenate([v] * (qrows // 8), axis=0)

    limit8 = by_row([len_ref[r] for r in range(local_rows)])
    freq = jnp.exp((lane8 % (HD // 2)).astype(F32) * (-2.0 * math.log(rope_base) / HD))
    angle = limit8.astype(F32) * freq
    cos_ref[...] = jnp.cos(angle)
    sin_ref[...] = jnp.where(lane8 < HD // 2, -1.0, 1.0) * jnp.sin(angle)
    for k in range(KVH):
        for u in range(blocks):
            for ref, table in ((ks_ref, kfac), (vs_ref, vfac)):
                power = by_row([ref[r, u, k] for r in range(local_rows)]).astype(F32)
                table[k * blocks + u] = jnp.exp2(power).astype(BF16).astype(F32)

    wkv_copy.wait()

    def turn(i, carry):
        start = pl.multiple_of(i * width, width)
        turned = jnp.transpose(wkv[:, pl.ds(start, width)].astype(F32)).astype(BF16)
        wq[pl.ds(start, width), qcols:] = turned
        return carry
    lax.fori_loop(0, n, turn, 0)
    others(lambda o: ss_copy(o, o).wait_recv())
    total_sq = jnp.sum(sbuf[...], axis=0)[0:1, :]
    column = jnp.transpose(jnp.broadcast_to(total_sq, (128, 128)))[0:rows, 0:1]
    scale = lax.rsqrt(column * (1.0 / (n * width)) + norm_eps)
    gain_copy.wait()

    def project(block):
        wq_copy(block).wait()
        start = pl.multiple_of(block * width, width)
        normed = (xbuf[block].astype(F32) * scale * gain_ref[:, pl.ds(start, width)]).astype(BF16)
        accq[...] += jnp.dot(normed, wq[pl.ds(start, width), :], preferred_element_type=F32)

    def take_line(m, h):
        @pl.when(m < line)
        def _():
            pos = ranked(m)
            ag_wait(at(pos, b, c), h)
            spread_line(pos, h)

    def take_pair(m, h):
        pos = ranked(m)
        block = at(pos, 1 - b, c)
        ag_wait(block, h)
        ag_copy(block, h, ag_core.at[2 * (line + pos) + h], cpeer).start()

    project(me)

    def gather_step(m, carry):
        take_line(m, 0)
        take_pair(m - 1, 0)
        cblock = at(ranked(m - 1), b, 1 - c)
        for h in range(2):
            ag_wait(cblock, h)
        project(cblock)
        take_line(m, 1)
        take_pair(m - 1, 1)
        project(at(ranked(m - 1), 1 - b, c))

        @pl.when(m < line)
        def _():
            project(at(ranked(m), b, c))

        @pl.when(m > 1)
        def _():
            block = at(ranked(m - 2), 1 - b, 1 - c)
            for h in range(2):
                ag_wait(block, h)
            project(block)

        @pl.when(m == 1)
        def _():
            kc_copy.start()
            vc_copy.start()
            for i in range(wo_parts):
                wo_copy(i).start()
        return carry
    lax.fori_loop(1, line + 1, gather_step, 0)
    last = at(ranked(line - 1), 1 - b, 1 - c)
    for h in range(2):
        ag_wait(last, h)
    project(last)

    pk[...] = jnp.zeros_like(pk)
    q_all = accq[...]
    kv_all = q_all[:, qcols:qcols + kv_cols]
    for j in range(n):
        mine = slice(j * local_rows, (j + 1) * local_rows)
        for g in range(own_heads):
            pk[j, g * local_rows:(g + 1) * local_rows, :] = q_all[mine, g * HD:(g + 1) * HD]
        pk[j, own_heads * local_rows:tile, 0:kv_cols] = kv_all[mine, :]
    qsend[...] = pk[...].astype(BF16)

    def q_copy(o, slot):
        return remote(qsend.at[o], qbuf.at[slot], q_send.at[o], q_recv.at[slot], o)

    others(lambda o: q_copy(o, me).start())
    qbuf[me] = qsend[me]

    limit = tall(limit8)
    lane = lax.broadcasted_iota(jnp.int32, (qrows, 128), 1)
    cosine, sine = tall(cos_ref[...]), tall(sin_ref[...])

    def rotated(v):
        return (v * cosine + pltpu.roll(v, HD // 2, 1) * sine).astype(BF16)

    kc_copy.wait()
    vc_copy.wait()
    others(lambda o: q_copy(o, o).wait_recv())

    pieces = HD // kv_cols
    factor = HD ** (-0.5)

    def new_head(first):
        res = None
        for p in range(pieces):
            part = jnp.dot(pick, qbuf[first + p], preferred_element_type=F32)
            part = part if p == 0 else pltpu.roll(part, p * kv_cols, 1)
            res = part if res is None else res + part
        return res

    for k in range(KVH):
        at_k = slice(k * HD, (k + 1) * HD)
        query = rotated(qbuf[k * per_head:(k + 1) * per_head].astype(F32).reshape(qrows, HD))
        new_key = rotated(new_head(k * pieces)).astype(F32)
        new_value = new_head((KVH + k) * pieces)
        own = jnp.sum(query.astype(F32) * new_key, axis=1, keepdims=True) * factor
        score = None
        for r in range(local_rows):
            one = lax.dot_general(query, kc[r, :, at_k], CONTRACT_LAST, preferred_element_type=F32)
            cut = [one[:, 128 * u:128 * (u + 1)] for u in range(blocks)]
            score = cut if r == 0 else [jnp.where(ridx == r, x, y) for x, y in zip(cut, score)]
        highest = None
        for u in range(blocks):
            scales = tall(kfac[k * blocks + u])
            score[u] = jnp.where(lane + 128 * u < limit, score[u] * scales * factor, -jnp.inf)
            highest = score[u] if u == 0 else jnp.maximum(highest, score[u])
        top = jnp.maximum(own, jnp.max(highest, axis=1, keepdims=True))
        own_weight = jnp.exp(own - top)
        added = None
        weights = []
        for u in range(blocks):
            weight = jnp.exp(score[u] - top)
            added = weight if u == 0 else added + weight
            scales = tall(vfac[k * blocks + u])
            weights.append((weight.astype(BF16).astype(F32) * scales).astype(BF16))
        total = own_weight + jnp.sum(added, axis=1, keepdims=True)
        weights = jnp.concatenate(weights, axis=1)
        summed = None
        for r in range(local_rows):
            one = jnp.dot(weights, vc[r, :, at_k], preferred_element_type=F32)
            summed = one if r == 0 else jnp.where(ridx == r, one, summed)
        summed = summed + own_weight.astype(BF16).astype(F32) * new_value
        result = (summed / total).astype(BF16)
        for s in range(per_head):
            asend[k * per_head + s] = result[s * tile:(s + 1) * tile, :]

    def a_copy(o, slot):
        return remote(asend.at[o], abuf.at[slot], a_send.at[o], a_recv.at[slot], o)

    others(lambda o: a_copy(o, me).start())
    abuf[me] = asend[me]
    for i in range(wo_parts):
        wo_copy(i).wait()
    others(lambda o: a_copy(o, o).wait_recv())
    pk[...] = abuf[...].astype(F32)
    for j in range(n):
        for g in range(own_heads):
            heads[j * local_rows:(j + 1) * local_rows, g * HD:(g + 1) * HD] = (
                pk[j, g * local_rows:(g + 1) * local_rows, :]
            )
    attended = heads[...].astype(BF16)

    def partial(block):
        start = pl.multiple_of(block * width, width)
        return jnp.dot(attended, wo[:, pl.ds(start, width)], preferred_element_type=F32)

    def core_copy(slot):
        return remote(core_sb.at[slot], core_rb.at[slot], core_send.at[slot], core_recv.at[slot], cpeer)

    def half_of(ref, pos, h):
        return ref.at[pos, pl.ds(h * half_rows, half_rows)]

    def y_copy(pos, h):
        i = 2 * pos + h
        return remote(half_of(y_sb, pos, h), half_of(y_rb, pos, h), y_send.at[i], y_recv.at[i], ypeer)

    def up_copy(pos, h):
        i = 2 * pos + h
        return remote(half_of(z_sb, pos, h), half_of(up_rb, pos, h), z_send.at[i], up_recv.at[i], up)

    def dn_copy(pos, h):
        i = 2 * pos + h
        return remote(half_of(z_sb, pos, h), half_of(dn_rb, pos, h), z_send.at[i], dn_recv.at[i], down)

    def to_core_far(pos):
        core_sb[line + pos] = partial(at(pos, 1 - b, 1 - c)).astype(BF16)
        core_copy(line + pos).start()

    def to_pair(pos):
        term = partial(at(pos, 1 - b, c))
        core_copy(line + pos).wait_recv()
        y_sb[pos] = (term + core_rb[line + pos].astype(F32)).astype(BF16)
        for h in range(2):
            y_copy(pos, h).start()

    def to_core_near(pos):
        core_sb[pos] = partial(at(pos, b, 1 - c)).astype(BF16)
        core_copy(pos).start()

    def to_line(pos):
        term = partial(at(pos, b, c))
        core_copy(pos).wait_recv()
        heads_sum[...] = term + core_rb[pos].astype(F32)
        for h in range(2):
            part = pl.ds(h * half_rows, half_rows)
            y_copy(pos, h).wait_recv()
            heads_sum[part] += y_rb[pos, part].astype(F32)

            @pl.when((pos >= a) & (a > 0))
            def _():
                up_copy(pos, h).wait_recv()
                heads_sum[part] += up_rb[pos, part].astype(F32)

            @pl.when((pos <= a) & (a < line - 1))
            def _():
                dn_copy(pos, h).wait_recv()
                heads_sum[part] += dn_rb[pos, part].astype(F32)

            @pl.when(pos > a)
            def _():
                z_sb[pos, part] = heads_sum[part].astype(BF16)
                up_copy(pos, h).start()

            @pl.when(pos < a)
            def _():
                z_sb[pos, part] = heads_sum[part].astype(BF16)
                dn_copy(pos, h).start()

            @pl.when(pos == a)
            def _():
                out_ref[part] = (x_ref[part].astype(F32) + heads_sum[part]).astype(BF16)

    def far(m):
        return ranked(line - 1 - m)

    to_core_far(far(0))

    def pair_step(m, carry):
        @pl.when(m + 1 < line)
        def _():
            to_core_far(far(m + 1))

        to_pair(far(m))
        return carry
    lax.fori_loop(0, line, pair_step, 0)

    to_core_near(far(0))

    def sum_step(m, carry):
        @pl.when(m + 1 < line)
        def _():
            to_core_near(far(m + 1))

        to_line(far(m))
        return carry
    lax.fori_loop(0, line, sum_step, 0)

    def sent_gather(i, carry):
        pos, h = i // 2, i % 2
        block = at(pos, b, c)

        @pl.when((pos <= a) & (a < line - 1))
        def _():
            ag_copy(block, h, ag_up.at[2 * pos + h], up).wait_send()

        @pl.when((pos >= a) & (a > 0))
        def _():
            ag_copy(block, h, ag_dn.at[2 * pos + h], down).wait_send()

        ag_copy(block, h, ag_y.at[2 * pos + h], ypeer).wait_send()
        ag_copy(block, h, ag_core.at[2 * pos + h], cpeer).wait_send()
        ag_copy(at(pos, 1 - b, c), h, ag_core.at[2 * (line + pos) + h], cpeer).wait_send()
        y_copy(pos, h).wait_send()

        @pl.when(pos > a)
        def _():
            up_copy(pos, h).wait_send()

        @pl.when(pos < a)
        def _():
            dn_copy(pos, h).wait_send()
        return carry
    lax.fori_loop(0, 2 * line, sent_gather, 0)

    def sent(pos, carry):
        core_copy(pos).wait_send()
        core_copy(line + pos).wait_send()
        return carry
    lax.fori_loop(0, line, sent, 0)

    def sent_others(o):
        ss_copy(o, o).wait_send()
        q_copy(o, o).wait_send()
        a_copy(o, o).wait_send()
    others(sent_others)


def fused_device(
    n, stream, norm_gain, w_query, w_keyval, w_out, lengths, key_cache, value_cache,
    key_scales, value_scales,
):
    rows, width = stream.shape
    local_rows = lengths.shape[0]
    span = key_cache.shape[1]
    line = n // 4
    qcols = w_query.shape[1]
    tile = (qcols // HD + 1) * local_rows
    vmem = pl.BlockSpec(memory_space=pltpu.VMEM)
    smem = pl.BlockSpec(memory_space=pltpu.SMEM)
    hbm = pl.BlockSpec(memory_space=pl.ANY)
    block = (rows, width)
    dma = pltpu.SemaphoreType.DMA
    return pl.pallas_call(
        functools.partial(fused_kernel, n, rows, width, local_rows, span),
        out_shape=jax.ShapeDtypeStruct(block, BF16),
        in_specs=[smem] * 3 + [hbm] * 7,
        out_specs=vmem,
        scratch_shapes=[
            pltpu.VMEM(block, BF16),
            pltpu.VMEM((1, n * width), F32),
            pltpu.VMEM((8, HD), F32),
            pltpu.VMEM((8, HD), F32),
            pltpu.VMEM((KVH * (span // 128), 8, 128), F32),
            pltpu.VMEM((KVH * (span // 128), 8, 128), F32),
            pltpu.VMEM((n * width, qcols + HD), BF16),
            pltpu.VMEM((HD, n * width), BF16),
            pltpu.VMEM(w_out.shape, BF16),
            pltpu.VMEM(key_cache.shape, BF16),
            pltpu.VMEM(value_cache.shape, BF16),
            pltpu.VMEM((n,) + block, BF16),
            pltpu.VMEM((8, 128), F32),
            pltpu.VMEM((n, 8, 128), F32),
            pltpu.VMEM((rows, qcols + HD), F32),
            pltpu.VMEM((n, tile, HD), F32),
            pltpu.VMEM((n, tile, HD), BF16),
            pltpu.VMEM((n, tile, HD), BF16),
            pltpu.VMEM((n, tile, HD), BF16),
            pltpu.VMEM((n, tile, HD), BF16),
            pltpu.VMEM((rows, qcols), F32),
            pltpu.VMEM((2 * line,) + block, BF16),
            pltpu.VMEM((2 * line,) + block, BF16),
            pltpu.VMEM((line,) + block, BF16),
            pltpu.VMEM((line,) + block, BF16),
            pltpu.VMEM((line,) + block, BF16),
            pltpu.VMEM((line,) + block, BF16),
            pltpu.VMEM((line,) + block, BF16),
            pltpu.VMEM(block, F32),
            dma((n,)), dma((4,)), dma((5,)),
            dma((2 * n,)), dma((2 * line,)), dma((2 * line,)), dma((2 * line,)), dma((4 * line,)),
            dma((n,)), dma((n,)), dma((n,)), dma((n,)), dma((n,)), dma((n,)),
            dma((2 * line,)), dma((2 * line,)), dma((2 * line,)), dma((2 * line,)), dma((2 * line,)),
            dma((2 * line,)), dma((2 * line,)),
        ],
        compiler_params=pltpu.CompilerParams(
            collective_id=0, has_side_effects=True, vmem_limit_bytes=62 * 2**20
        ),
        cost_estimate=pl.CostEstimate(
            flops=4 * rows * w_query.size, bytes_accessed=4 * w_query.size, transcendentals=0
        ),
    )(
        lengths, key_scales, value_scales, stream, norm_gain.reshape(1, -1),
        w_query, w_keyval.T, w_out, key_cache, value_cache,
    )


def per_device(n, *args):
    stream, _, w_query, w_keyval, _, lengths, key_cache, *_ = args
    rows, width = stream.shape
    local_rows = lengths.shape[0]
    qcols, kv_cols = w_query.shape[1], w_keyval.shape[1]
    tiles = (
        n % 4 == 0 and n >= 8 and n % KVH == 0 and width % 128 == 0 and qcols % HD == 0
        and HD % kv_cols == 0 and rows % 32 == 0 and rows <= 128
        and 8 % local_rows == 0
        and (qcols // HD + 1) * local_rows % 16 == 0
        and key_cache.shape[1] // 128 == args[8].shape[1]
    )
    return fused_device(n, *args) if tiles else plain_device(*args)


def solution(mesh):
    return jax.shard_map(
        functools.partial(per_device, mesh.shape["out"]),
        mesh=mesh,
        in_specs=(
            P("groups", "out"),
            P(),
            P(None, "out"),
            P(None, "out"),
            P("out", None),
            P(("groups", "out")),
            P(("groups", "out"), None, None),
            P(("groups", "out"), None, None),
            P(("groups", "out"), None, None),
            P(("groups", "out"), None, None),
        ),
        out_specs=P("groups", "out"),
        check_vma=False,
    )
```
